1024 devices in a mesh: dp: 16 (over x, core), loss: 16 (over z_lo, y), mp: 4 (over z_hi).
Axes of the slice: x: 8, y: 8, z: 8 (z_hi: 4, z_lo: 2; z = z_hi * 2 + z_lo), core: 2. Of those that a mesh axis runs over, the one named last changes fastest.
Arguments:
- patches: bfloat16 [81920, 1152], P(('dp', 'loss'))
- layer_norm_gain: float32 [1152], replicated, may hold values from 0.5 to 1.5
- layer_norm_bias: float32 [1152], replicated, may hold values from -1.75 to 1.75
- fc1_weight: bfloat16 [1152, 4304], P(None, 'mp'), may hold values from -0.1875 to 0.1875
- fc1_bias: float32 [4304], P('mp'), may hold values from -1.75 to 1.75
- fc2_weight: bfloat16 [4304, 1152], P('mp'), may hold values from -0.09375 to 0.09375
- counts: int32 [16, 8], P('loss'), may hold values from 256 to 1024, as said below
- owners: int32 [16, 16, 16], P('loss'), may hold values from 0 to 15, each once within a row
- text_embed: bfloat16 [128, 1152], P('loss'), may hold values from -0.1875 to 0.1875
- labels: int32 [128], replicated, may hold values from 0 to 127, each once
- logit_scale: float32 [1], replicated, may hold values from 5 to 20
- logit_bias: float32 [1], replicated, may hold values from -6 to -3
Outputs:
- grad_rows: float32 [81920, 1152], P(('dp', 'loss', 'mp'))
- grad_text: float32 [128, 1152], P('loss')
- loss: float32 [], replicated
The draws below stay inside these ranges and needn't reach their ends.
Inputs may be any that keep to these rules, and one draw needn't show every extreme that they name: In each pair group the counts add up to 5120; one image of every group has exactly 1024 patches and one exactly 256. For each group and source, the owners of the 16 blocks are all different. `labels`: each text matches exactly one image.
All inputs are finite; a program needn't handle non-finite values.
Results may differ from the reference program's by a relative error of at most 0.015.
Values may be sent and summed in bfloat16 or wider, within the bound.
No kernel may reach another device: no remote copies, remote signals or barrier semaphores. Data moves between devices by JAX's collectives and lax.ppermute only.
A program may use at most 32 MiB of HBM per device.

```python
import math
import jax
import jax.numpy as jnp
from jax import lax

D = 1152
FF = 4304
ROWS = 320
PMIN = 256
PMAX = 1024
BLK = 20
PACK = 5120
NIMG = 8
IMAGES = 128
N_DP = 16
N_LOSS = 16
N_MP = 4


def draw_patches(key, part):
    key = jax.random.fold_in(key, 11)
    key_noise, key_level, key_scale = jax.random.split(key, 3)
    total_rows = N_DP * N_LOSS * ROWS
    level_rows = total_rows // BLK
    noise = jax.random.normal(key_noise, (total_rows, D), jnp.float32)
    level = 1.5 * jax.random.normal(key_level, (level_rows, D), jnp.float32)
    row_scale = jnp.exp(jax.random.uniform(key_scale, (total_rows, 1), jnp.float32, -1.2, 1.1))
    full = (noise + jnp.repeat(level, BLK, axis=0)) * row_scale
    return full.astype(jnp.bfloat16)


def draw_counts(key, part):
    key = jax.random.fold_in(key, 23)
    key_shift, key_order = jax.random.split(key, 2)
    half_count = NIMG // 2
    shifts = jax.random.randint(key_shift, (N_LOSS, half_count), 0, PMAX - PMIN + 1)
    shifts = shifts.at[:, 0].set(0)
    paired = jnp.stack([PMIN + shifts, PMAX - shifts], axis=-1).reshape(N_LOSS, NIMG)
    scores = jax.random.randint(key_order, (N_LOSS, NIMG), 0, 1048576) * NIMG + jnp.arange(NIMG, dtype=jnp.int32)[None, :]
    order = jnp.argsort(scores, axis=-1)
    return jnp.take_along_axis(paired, order, axis=1).astype(jnp.int32)


def level_of(own_key, shape, pieces, smallest, largest):
    def one(axis_at, parts):
        draws = jax.random.uniform(jax.random.fold_in(jax.random.fold_in(own_key, 6), axis_at), (parts,), jnp.float32, smallest / len(pieces), largest / len(pieces))
        return jnp.repeat(jnp.exp(draws), shape[axis_at] // parts).reshape((-1,) + (1,) * (len(shape) - axis_at - 1))

    loudness = one(*pieces[0])
    for cut in pieces[1:]:
        loudness = loudness * one(*cut)
    return loudness


def centred(own_key, dims, scale, limit, shards=(), kind=jnp.bfloat16):
    level = level_of(own_key, dims, shards, -0.22, 0.18) if shards else 1.0
    values = jax.random.normal(own_key, dims, jnp.float32) * scale * level
    return jnp.minimum(jnp.maximum(values, -limit), limit).astype(kind)


def setup_inputs(seed: int = 0) -> dict:
    streams_of = jax.random.split(jax.random.key(seed), 13)
    return {
        "patches": draw_patches(jax.random.fold_in(streams_of[12], 71), 0),
        "layer_norm_gain": jnp.clip(1.0 + 0.1 * jax.random.normal(streams_of[1], (D,), jnp.float32), 0.5, 1.5),
        "layer_norm_bias": centred(streams_of[2], (D,), 0.3, 1.75, (), jnp.float32),
        "fc1_weight": centred(streams_of[3], (D, FF), D ** -0.5, 0.1875, ((1, 4),)),
        "fc1_bias": centred(streams_of[4], (FF,), 0.3, 1.75, ((0, 4),), jnp.float32),
        "fc2_weight": centred(streams_of[5], (FF, D), FF ** -0.5, 0.09375, ((0, 4),)),
        "counts": draw_counts(jax.random.fold_in(streams_of[12], 71), 0),
        "owners": jax.vmap(lambda own: jax.random.permutation(own, N_DP))(jax.random.split(streams_of[7], N_LOSS * N_DP)).reshape((N_LOSS, N_DP, N_DP)).astype(jnp.int32),
        "text_embed": centred(streams_of[8], (IMAGES, D), 0.03, 0.1875, ((0, 16),)),
        "labels": jax.random.permutation(streams_of[9], IMAGES).astype(jnp.int32),
        "logit_scale": jnp.clip(jnp.exp(jax.random.uniform(streams_of[10], (1,), jnp.float32, math.log(5.0), math.log(20.0))), 5.0, 20.0),
        "logit_bias": jnp.clip(jax.random.uniform(streams_of[11], (1,), jnp.float32, -6.0, -3.0), -6.0, -3.0),
    }


eps = 1e-06
grad_scale = 262144.0
gelu_coef = 0.7978845608028654

def gelu_tanh(values):
    inner = gelu_coef * (values + 0.044715 * values * values * values)
    return 0.5 * values * (1.0 + jnp.tanh(inner))

def gelu_slope(values):
    inner = gelu_coef * (values + 0.044715 * values * values * values)
    tanh_part = jnp.tanh(inner)
    return 0.5 * (1.0 + tanh_part) + 0.5 * values * (1.0 - tanh_part * tanh_part) * gelu_coef * (1.0 + 0.134145 * values * values)

def layer_statistics(rows_in):
    floats = rows_in.astype(jnp.float32)
    center = floats - lax.optimization_barrier(jnp.mean(floats, axis=-1, keepdims=True))
    spread = lax.optimization_barrier(jnp.mean(center * center, axis=-1, keepdims=True))
    inverse_deviation = lax.rsqrt(spread + eps)
    return (center * inverse_deviation, inverse_deviation)

def membership(count_row):
    position = jnp.arange(PACK, dtype=jnp.int32)
    ends = jnp.cumsum(count_row).astype(jnp.int32)
    starts = ends - count_row
    inside = (position[:, None] >= starts[None, :]) & (position[:, None] < ends[None, :])
    return inside.astype(jnp.float32)

def reference(patches, layer_norm_gain, layer_norm_bias, fc1_weight, fc1_bias, fc2_weight, counts, owners, text_embed, labels, logit_scale, logit_bias):
    groups = patches.reshape(N_DP, N_LOSS, ROWS, D).transpose(1, 0, 2, 3).reshape(N_LOSS, PACK, D)
    slab = FF // N_MP

    def forward_group(items):
        rows_of_group, count_row = items
        normalized_input, inverse_deviation = layer_statistics(rows_of_group)
        normalized_rows = (normalized_input * layer_norm_gain + layer_norm_bias).astype(jnp.bfloat16)
        mixed = jnp.zeros((PACK, D), jnp.float32)
        for piece in range(N_MP):
            pre = jnp.dot(normalized_rows, fc1_weight[:, piece * slab:(piece + 1) * slab], preferred_element_type=jnp.float32) + fc1_bias[piece * slab:(piece + 1) * slab]
            act = gelu_tanh(pre).astype(jnp.bfloat16)
            part = jnp.dot(act, fc2_weight[piece * slab:(piece + 1) * slab], preferred_element_type=jnp.float32).astype(jnp.bfloat16)
            part = lax.optimization_barrier(part)
            mixed = mixed + part.astype(jnp.float32)
        output = rows_of_group.astype(jnp.float32) + mixed
        member = membership(count_row)
        sums = jnp.dot(member.T, output, precision=lax.Precision.HIGHEST)
        return sums / count_row.astype(jnp.float32)[:, None]
    embeds = lax.map(forward_group, (groups, counts)).reshape(IMAGES, D)
    norm_e = jnp.sqrt(lax.optimization_barrier(jnp.sum(embeds * embeds, axis=-1, keepdims=True)) + eps)
    unit_e = embeds / norm_e
    texts = text_embed.astype(jnp.float32)
    norm_t = jnp.sqrt(lax.optimization_barrier(jnp.sum(texts * texts, axis=-1, keepdims=True)) + eps)
    unit_t = texts / norm_t
    score = logit_scale[0] * jnp.dot(unit_e, unit_t.T, precision=lax.Precision.HIGHEST) + logit_bias[0]
    sign = jnp.where(labels[:, None] == jnp.arange(IMAGES, dtype=jnp.int32)[None, :], 1.0, -1.0).astype(jnp.float32)
    loss = -jnp.sum(jax.nn.log_sigmoid(sign * score)) / IMAGES
    dscore = -sign * jax.nn.sigmoid(-sign * score) / IMAGES
    d_unit_e = logit_scale[0] * jnp.dot(dscore, unit_t, precision=lax.Precision.HIGHEST)
    d_unit_t = logit_scale[0] * jnp.dot(dscore.T, unit_e, precision=lax.Precision.HIGHEST)
    dembed = (d_unit_e - unit_e * lax.optimization_barrier(jnp.sum(unit_e * d_unit_e, axis=-1, keepdims=True))) / norm_e
    grad_text = (d_unit_t - unit_t * lax.optimization_barrier(jnp.sum(unit_t * d_unit_t, axis=-1, keepdims=True))) / norm_t

    def backward_group(items):
        rows_of_group, count_row, dembed_group = items
        normalized_input, inverse_deviation = layer_statistics(rows_of_group)
        normalized_rows = (normalized_input * layer_norm_gain + layer_norm_bias).astype(jnp.bfloat16)
        member = membership(count_row)
        upstream = grad_scale * jnp.dot(member, dembed_group / count_row.astype(jnp.float32)[:, None], precision=lax.Precision.HIGHEST)
        upstream_b = upstream.astype(jnp.bfloat16)
        backward_pass = jnp.zeros((PACK, D), jnp.float32)
        for piece in range(N_MP):
            w_first = fc1_weight[:, piece * slab:(piece + 1) * slab]
            w_second = fc2_weight[piece * slab:(piece + 1) * slab]
            pre = jnp.dot(normalized_rows, w_first, preferred_element_type=jnp.float32) + fc1_bias[piece * slab:(piece + 1) * slab]
            d_act = jnp.dot(upstream_b, w_second.T, preferred_element_type=jnp.float32)
            d_pre = (d_act * gelu_slope(pre)).astype(jnp.bfloat16)
            part = jnp.dot(d_pre, w_first.T, preferred_element_type=jnp.float32).astype(jnp.bfloat16)
            part = lax.optimization_barrier(part)
            backward_pass = backward_pass + part.astype(jnp.float32)
        normalized_gradient = backward_pass * layer_norm_gain
        row_gradients = inverse_deviation * (normalized_gradient - lax.optimization_barrier(jnp.mean(normalized_gradient, axis=-1, keepdims=True)) - normalized_input * lax.optimization_barrier(jnp.mean(normalized_gradient * normalized_input, axis=-1, keepdims=True)))
        return row_gradients + upstream
    grads = lax.map(backward_group, (groups, counts, dembed.reshape(N_LOSS, NIMG, D)))
    grads = grads.reshape(N_LOSS, N_DP, N_DP, BLK, D)
    inverse = jnp.argsort(owners, axis=-1).astype(jnp.int32)
    group_index = jnp.arange(N_LOSS, dtype=jnp.int32)[:, None, None]
    source_index = jnp.arange(N_DP, dtype=jnp.int32)[None, :, None]
    picked = grads[group_index, source_index, inverse]
    grad_rows = picked.transpose(2, 0, 1, 3, 4).reshape(N_DP * N_LOSS * ROWS, D)
    return (grad_rows, grad_text, loss)
```

```python
import functools

import jax
import jax.numpy as jnp
from jax import lax
from jax.experimental import pallas as pl
from jax.experimental.pallas import tpu as pltpu
from jax.sharding import PartitionSpec as P

eps = 1e-06
grad_scale = 262144.0
gelu_coef = 0.7978845608028654
f32 = jnp.float32
bf16 = jnp.bfloat16
VMEM_LIMIT = 48 * 1024 * 1024
whole = pl.BlockSpec(memory_space=pltpu.VMEM)
scalars = pl.BlockSpec(memory_space=pltpu.SMEM)
NT = (((1,), (1,)), ((), ()))
TN = (((0,), (0,)), ((), ()))
HIGHEST = lax.Precision.HIGHEST


def column_chunks(width, step):
    return [(first, min(step, width - first)) for first in range(0, width, step)]


def layer_statistics(floats):
    center = floats - jnp.mean(floats, axis=-1, keepdims=True)
    spread = jnp.mean(center * center, axis=-1, keepdims=True)
    inverse_deviation = lax.rsqrt(spread + eps)
    return center * inverse_deviation, inverse_deviation


def split_bf16(values):
    high = values.astype(bf16)
    return high, (values - high.astype(f32)).astype(bf16)


def pool_kernel(dp_ref, counts_ref, x_ref, gain_ref, bias_ref, w1_ref, b1_ref, w2_ref, out_ref, *, share):
    rows = x_ref.shape[0]
    images = counts_ref.shape[1]
    position = dp_ref[0] * rows + lax.broadcasted_iota(jnp.int32, (images, rows), 1)
    image = lax.broadcasted_iota(jnp.int32, (images, rows), 0)
    member = jnp.zeros((images, rows), f32)
    start = jnp.int32(0)
    for j in range(images):
        end = start + counts_ref[0, j]
        inside = (image == j) & (position >= start) & (position < end)
        member = jnp.where(inside, 1.0, member)
        start = end
    member = member.astype(bf16)
    x = x_ref[...]
    xhat, _ = layer_statistics(x.astype(f32))
    normed = (xhat * gain_ref[...] + bias_ref[...]).astype(bf16)
    total = share * jnp.dot(member, x, preferred_element_type=f32)
    for first, many in column_chunks(w1_ref.shape[1], 256):
        cols = slice(first, first + many)
        pre = jnp.dot(normed, w1_ref[:, cols], preferred_element_type=f32) + b1_ref[:, cols]
        inner = gelu_coef * (pre + 0.044715 * pre * pre * pre)
        act = (0.5 * pre * (1.0 + jnp.tanh(inner))).astype(bf16)
        pooled = jnp.dot(member, act, preferred_element_type=f32)
        w2 = w2_ref[cols, :]
        for piece in split_bf16(pooled):
            total = total + jnp.dot(piece, w2, preferred_element_type=f32)
    out_ref[...] = total


def slope_kernel(x_ref, gain_ref, bias_ref, w1_ref, b1_ref, slope_ref):
    xhat, _ = layer_statistics(x_ref[...].astype(f32))
    normed = (xhat * gain_ref[...] + bias_ref[...]).astype(bf16)
    for first, many in column_chunks(w1_ref.shape[1], 256):
        cols = slice(first, first + many)
        pre = jnp.dot(normed, w1_ref[:, cols], preferred_element_type=f32) + b1_ref[:, cols]
        square = pre * pre
        tanh_part = jnp.tanh(gelu_coef * (pre + 0.044715 * square * pre))
        slope_ref[:, cols] = 0.5 * (1.0 + tanh_part) + 0.5 * pre * (
            1.0 - tanh_part * tanh_part
        ) * gelu_coef * (1.0 + 0.134145 * square)


def unit_rows(values):
    norm = jnp.sqrt(jnp.sum(values * values, axis=-1, keepdims=True) + eps)
    return values / norm, norm


def embed_kernel(pieces_ref, counts_ref, texts_ref, matches_ref, scale_ref, shift_ref, embed_ref, upstream_ref):
    total = pieces_ref[0]
    for k in range(1, pieces_ref.shape[0]):
        total = total + pieces_ref[k]
    counts = counts_ref[...]
    embed = total / counts
    embed_ref[...] = embed.astype(bf16)
    unit_e, norm_e = unit_rows(embed)
    unit_t, _ = unit_rows(texts_ref[...].astype(f32))
    images = unit_t.shape[0]
    scale = scale_ref[0]
    score = scale * lax.dot_general(unit_e, unit_t, NT, precision=HIGHEST, preferred_element_type=f32) + shift_ref[0]
    sign = 2.0 * matches_ref[...] - 1.0
    dscore = -sign * jax.nn.sigmoid(-sign * score) / images
    du = scale * jnp.dot(dscore, unit_t, precision=HIGHEST, preferred_element_type=f32)
    dembed = (du - unit_e * jnp.sum(unit_e * du, axis=-1, keepdims=True)) / norm_e
    upstream_ref[...] = grad_scale * (dembed / counts)


def back_kernel(upstream_ref, member_ref, slope_ref, w1_ref, w2_ref, out_ref):
    d_image = upstream_ref[...].astype(bf16)
    d_act = lax.dot_general(d_image, w2_ref[...], NT, preferred_element_type=f32)
    member = member_ref[...]
    high, low = split_bf16(d_act)
    d_rows = jnp.dot(member, high, preferred_element_type=f32) + jnp.dot(member, low, preferred_element_type=f32)
    d_pre = (d_rows * slope_ref[...]).astype(bf16)
    out_ref[...] = lax.dot_general(d_pre, w1_ref[...], NT, preferred_element_type=f32).astype(bf16)


def row_kernel(own_ref, first_ref, second_ref, third_ref, x_ref, gain_ref, member_ref, upstream_ref, out_ref):
    back = own_ref[...].astype(f32) + first_ref[...].astype(f32)
    back = back + second_ref[...].astype(f32) + third_ref[...].astype(f32)
    xhat, inverse_deviation = layer_statistics(x_ref[...].astype(f32))
    dxhat = back * gain_ref[...]
    dx = inverse_deviation * (
        dxhat
        - jnp.mean(dxhat, axis=-1, keepdims=True)
        - xhat * jnp.mean(dxhat * xhat, axis=-1, keepdims=True)
    )
    upstream = jnp.dot(member_ref[...], upstream_ref[...], precision=HIGHEST, preferred_element_type=f32)
    out_ref[...] = dx + upstream


def loss_kernel(embeds_ref, texts_ref, own_text_ref, labels_ref, matches_ref, scale_ref, shift_ref, grad_ref, loss_ref):
    unit_e, _ = unit_rows(embeds_ref[...].astype(f32))
    unit_t, _ = unit_rows(texts_ref[...].astype(f32))
    images = unit_e.shape[0]
    scale = scale_ref[0]
    score = scale * lax.dot_general(unit_e, unit_t, NT, precision=HIGHEST, preferred_element_type=f32) + shift_ref[0]
    text_index = lax.broadcasted_iota(jnp.int32, (images, images), 1)
    sign = jnp.where(labels_ref[...] == text_index, 1.0, -1.0)
    margin = sign * score
    log_sigmoid = jnp.minimum(margin, 0.0) - jnp.log1p(jnp.exp(-jnp.abs(margin)))
    row_sums = jnp.sum(log_sigmoid, axis=1, keepdims=True)
    loss_ref[...] = -jnp.sum(row_sums, axis=0, keepdims=True) / images
    unit_o, norm_o = unit_rows(own_text_ref[...].astype(f32))
    own_score = scale * lax.dot_general(unit_o, unit_e, NT, precision=HIGHEST, preferred_element_type=f32) + shift_ref[0]
    own_sign = 2.0 * matches_ref[...] - 1.0
    dscore = -own_sign * jax.nn.sigmoid(-own_sign * own_score) / images
    dv = scale * jnp.dot(dscore, unit_e, precision=HIGHEST, preferred_element_type=f32)
    grad_ref[...] = (dv - unit_o * jnp.sum(unit_o * dv, axis=-1, keepdims=True)) / norm_o


def call(kernel, outs, specs, operands, flops=0, read=0):
    return pl.pallas_call(
        kernel,
        out_shape=outs,
        in_specs=specs,
        out_specs=jax.tree.map(lambda _: whole, outs),
        compiler_params=pltpu.CompilerParams(vmem_limit_bytes=VMEM_LIMIT),
        cost_estimate=pl.CostEstimate(flops=flops, bytes_accessed=read, transcendentals=0),
    )(*operands)


def shape(dims, kind):
    return jax.ShapeDtypeStruct(dims, kind)


def gather_by_exchange(block, axis):
    copies = jnp.broadcast_to(block[None], (lax.axis_size(axis),) + block.shape)
    return lax.all_to_all(copies, axis, split_axis=0, concat_axis=0, tiled=True)


def shards(
    patches,
    layer_norm_gain,
    layer_norm_bias,
    fc1_weight,
    fc1_bias,
    fc2_weight,
    counts,
    owners,
    text_embed,
    labels,
    logit_scale,
    logit_bias,
):
    dp_size = lax.axis_size("dp")
    mp_size = lax.axis_size("mp")
    dp_index = lax.axis_index("dp")
    mp_index = lax.axis_index("mp")
    loss_index = lax.axis_index("loss")
    row_count, width = patches.shape
    hidden = fc1_weight.shape[1]
    block_rows = row_count // dp_size
    share_rows = row_count // mp_size
    group_images = counts.shape[1]
    total_images = labels.shape[0]
    gain = layer_norm_gain[None, :]
    bias = layer_norm_bias[None, :]
    fc1_offset = fc1_bias[None, :]
    plan = owners[0]
    slots = jnp.arange(dp_size, dtype=jnp.int32)

    all_texts = gather_by_exchange(text_embed, "loss").reshape(total_images, width)

    mine = lax.dynamic_index_in_dim(plan, dp_index, 0, keepdims=False)
    order = jnp.sum(jnp.where(mine[None, :] == slots[:, None], slots[None, :], 0), axis=1)
    outgoing = patches.reshape(dp_size, block_rows, width)[order]
    incoming = lax.all_to_all(outgoing, "dp", split_axis=0, concat_axis=0, tiled=True)

    matmul = 2 * row_count * width * hidden
    partial_sums = call(
        functools.partial(pool_kernel, share=1.0 / mp_size),
        shape((group_images, width), f32),
        [scalars, scalars] + [whole] * 6,
        (dp_index[None].astype(jnp.int32), counts, patches, gain, bias, fc1_weight, fc1_offset, fc2_weight),
        flops=matmul,
        read=4 * width * hidden,
    )
    slab_pieces = lax.all_gather(partial_sums, "mp", axis=0)
    slab_sums = jnp.sum(slab_pieces, axis=0)
    pieces = lax.all_gather(slab_sums, "dp", axis=0)

    local_rows = incoming.reshape(row_count, width)
    source_block = jnp.sum(jnp.where(plan == dp_index, slots[None, :], 0), axis=1)
    position = (
        slots[:, None] * row_count
        + source_block[:, None] * block_rows
        + jnp.arange(block_rows, dtype=jnp.int32)[None, :]
    ).reshape(row_count)
    ends = jnp.cumsum(counts[0])
    starts = ends - counts[0]
    member = ((position[:, None] >= starts[None, :]) & (position[:, None] < ends[None, :])).astype(bf16)
    first_row = mp_index * share_rows
    own_rows = lax.dynamic_slice_in_dim(local_rows, first_row, share_rows, 0)
    own_member = lax.dynamic_slice_in_dim(member, first_row, share_rows, 0).astype(f32)
    slope = call(
        slope_kernel,
        shape((row_count, hidden), f32),
        [whole] * 5,
        (local_rows, gain, bias, fc1_weight, fc1_offset),
        flops=matmul,
        read=4 * width * hidden,
    )

    own_first = loss_index * group_images
    text_index = jnp.arange(total_images, dtype=jnp.int32)
    own_labels = lax.dynamic_slice_in_dim(labels, own_first, group_images, 0)
    image_matches = (own_labels[:, None] == text_index[None, :]).astype(f32)
    own_texts = own_first + jnp.arange(group_images, dtype=jnp.int32)
    text_matches = (labels[None, :] == own_texts[:, None]).astype(f32)
    counts_column = counts[0].astype(f32)[:, None]
    embed, upstream = call(
        embed_kernel,
        (shape((group_images, width), bf16), shape((group_images, width), f32)),
        [whole] * 4 + [scalars] * 2,
        (pieces, counts_column, all_texts, image_matches, logit_scale, logit_bias),
    )
    back = call(
        back_kernel,
        shape((row_count, width), bf16),
        [whole] * 5,
        (upstream, member, slope, fc1_weight, fc2_weight),
        flops=matmul,
        read=4 * width * hidden,
    )
    received = []
    for step in (2, 1, 3):
        peer = (mp_index + step) % mp_size
        chunk = lax.dynamic_slice_in_dim(back, peer * share_rows, share_rows, 0)
        pairs = [(i, (i + step) % mp_size) for i in range(mp_size)]
        received.append(lax.ppermute(chunk, "mp", pairs))
    all_embeds = gather_by_exchange(embed, "loss").reshape(total_images, width)
    grad_text, loss = call(
        loss_kernel,
        (shape((group_images, width), f32), shape((1, 1), f32)),
        [whole] * 5 + [scalars] * 2,
        (all_embeds, all_texts, text_embed, labels[:, None], text_matches, logit_scale, logit_bias),
    )
    own_back = lax.dynamic_slice_in_dim(back, first_row, share_rows, 0)
    grad_rows = call(
        row_kernel,
        shape((share_rows, width), f32),
        [whole] * 8,
        (own_back, *received, own_rows, gain, own_member, upstream),
    )
    return (grad_rows, grad_text, loss[0, 0])


def solution(mesh):
    placed = (
        P(("dp", "loss"), None),
        P(),
        P(),
        P(None, "mp"),
        P("mp"),
        P("mp", None),
        P("loss", None),
        P("loss", None, None),
        P("loss", None),
        P(),
        P(),
        P(),
    )
    return jax.shard_map(
        shards,
        mesh=mesh,
        in_specs=placed,
        out_specs=(P(("dp", "loss", "mp"), None), P("loss", None), P()),
        check_vma=False,
    )
```

```python
import functools

import jax
import jax.numpy as jnp
from jax import lax
from jax.experimental import pallas as pl
from jax.experimental.pallas import tpu as pltpu
from jax.sharding import PartitionSpec as P

eps = 1e-06
grad_scale = 262144.0
gelu_coef = 0.7978845608028654
f32 = jnp.float32
bf16 = jnp.bfloat16
VMEM_LIMIT = 48 * 1024 * 1024
whole = pl.BlockSpec(memory_space=pltpu.VMEM)
scalars = pl.BlockSpec(memory_space=pltpu.SMEM)
NT = (((1,), (1,)), ((), ()))
TN = (((0,), (0,)), ((), ()))
LANES = 128
HIGHEST = lax.Precision.HIGHEST


def column_chunks(width, step):
    return [(first, min(step, width - first)) for first in range(0, width, step)]


def layer_statistics(floats):
    center = floats - jnp.mean(floats, axis=-1, keepdims=True)
    spread = jnp.mean(center * center, axis=-1, keepdims=True)
    inverse_deviation = lax.rsqrt(spread + eps)
    return center * inverse_deviation, inverse_deviation


def split_bf16(values):
    high = values.astype(bf16)
    return high, (values - high.astype(f32)).astype(bf16)


def split_three(values):
    high, rest = split_bf16(values)
    return high, rest, (values - high.astype(f32) - rest.astype(f32)).astype(bf16)


def quotient(values, by):
    return (values * (65536 // by + 1)) >> 16


def iota(dims, axis):
    return lax.broadcasted_iota(jnp.int32, dims, axis)


def one_hot(condition):
    return jnp.where(condition, 1.0, 0.0).astype(bf16)


def pack_kernel(dp_ref, owners_ref, x_ref, text_ref, out_ref, copies_ref, *, padded):
    rows = x_ref.shape[0]
    slots = owners_ref.shape[0]
    block_rows = rows // slots
    block = quotient(iota((1, rows), 1), block_rows)
    within = iota((1, rows), 1) - block * block_rows
    owner = jnp.zeros((1, rows), jnp.int32)
    for b in range(slots):
        owner = jnp.where(block == b, owners_ref[dp_ref[0], b], owner)
    target = owner * padded + within
    pick = one_hot(iota((slots * padded, rows), 0) == target)
    out_ref[...] = jnp.dot(pick, x_ref[...], preferred_element_type=f32).astype(bf16)
    text = text_ref[...].astype(f32)
    copies_ref[...] = jnp.concatenate([text] * (copies_ref.shape[0] // text.shape[0]), axis=0).astype(bf16)


def image_bounds(counts_ref, dims, axis):
    image = iota(dims, axis)
    starts = jnp.zeros(dims, jnp.int32)
    ends = jnp.zeros(dims, jnp.int32)
    first = jnp.int32(0)
    for j in range(counts_ref.shape[1]):
        last = first + counts_ref[0, j]
        starts = jnp.where(image == j, first, starts)
        ends = jnp.where(image == j, last, ends)
        first = last
    return starts, ends


def pool_kernel(dp_ref, counts_ref, x_ref, gain_ref, bias_ref, w1t_ref, b1_ref, w2_ref, out_ref, *, share):
    rows = x_ref.shape[0]
    images = counts_ref.shape[1]
    position = dp_ref[0] * rows + iota((images, rows), 1)
    starts, ends = image_bounds(counts_ref, (images, 1), 0)
    member = one_hot((position >= starts) & (position < ends))
    x = x_ref[...]
    xhat, _ = layer_statistics(x.astype(f32))
    normed = (xhat * gain_ref[...][None, :] + bias_ref[...][None, :]).astype(bf16)
    offset = b1_ref[...][None, :]
    total = share * jnp.dot(member, x, preferred_element_type=f32)
    for first, many in column_chunks(w1t_ref.shape[0], 256):
        cols = slice(first, first + many)
        pre = lax.dot_general(normed, w1t_ref[cols, :], NT, preferred_element_type=f32) + offset[:, cols]
        inner = gelu_coef * (pre + 0.044715 * pre * pre * pre)
        act = (0.5 * pre * (1.0 + jnp.tanh(inner))).astype(bf16)
        pooled = jnp.dot(member, act, preferred_element_type=f32)
        both = jnp.concatenate(split_bf16(pooled), axis=0)
        product = jnp.dot(both, w2_ref[cols, :], preferred_element_type=f32)
        total = total + product[:images] + product[images:]
    out_ref[...] = total


def slope_kernel(
    dp_ref, counts_ref, owners_ref, in_ref, gain_ref, bias_ref, w1t_ref, b1_ref, slope_ref, rows_ref, member_ref
):
    rows = rows_ref.shape[0]
    slots = owners_ref.shape[0]
    block_rows = rows // slots
    padded = in_ref.shape[0] // slots
    source = quotient(iota((rows, 1), 0), block_rows)
    within = iota((rows, 1), 0) - source * block_rows
    pick = one_hot(iota((rows, in_ref.shape[0]), 1) == source * padded + within)
    x = jnp.dot(pick, in_ref[...], preferred_element_type=f32)
    rows_ref[...] = x.astype(bf16)
    block = jnp.where(owners_ref[...] == dp_ref[0], iota((slots, slots), 1), 0)
    block = jnp.sum(block.astype(f32), axis=1, keepdims=True)
    by_source = one_hot(iota((rows, slots), 1) == source)
    block = jnp.dot(by_source, jnp.broadcast_to(block, (slots, LANES)).astype(bf16), preferred_element_type=f32)
    position = source * rows + block[:, :1].astype(jnp.int32) * block_rows + within
    starts, ends = image_bounds(counts_ref, (1, member_ref.shape[1]), 1)
    member_ref[...] = jnp.where((position >= starts) & (position < ends), 1.0, 0.0)
    xhat, _ = layer_statistics(x)
    normed = (xhat * gain_ref[...][None, :] + bias_ref[...][None, :]).astype(bf16)
    offset = b1_ref[...][None, :]
    for first, many in column_chunks(w1t_ref.shape[0], 256):
        cols = slice(first, first + many)
        pre = lax.dot_general(normed, w1t_ref[cols, :], NT, preferred_element_type=f32) + offset[:, cols]
        square = pre * pre
        tanh_part = jnp.tanh(gelu_coef * (pre + 0.044715 * square * pre))
        slope_ref[:, cols] = 0.5 * (1.0 + tanh_part) + 0.5 * pre * (
            1.0 - tanh_part * tanh_part
        ) * gelu_coef * (1.0 + 0.134145 * square)


def log_sigmoid(values):
    return jnp.minimum(values, 0.0) - jnp.log1p(jnp.exp(-jnp.abs(values)))


def embed_kernel(
    loss_ref, counts_ref, labels_ref, scale_ref, shift_ref, pieces_ref, texts_ref, upstream_ref, parts_ref
):
    total = pieces_ref[0]
    for k in range(1, pieces_ref.shape[0]):
        total = total + pieces_ref[k]
    images, width = total.shape
    texts = texts_ref[...]
    all_images = texts.shape[0]
    image = iota((images, 1), 0)
    count = jnp.zeros((images, 1), jnp.int32)
    label = jnp.zeros((images, 1), jnp.int32)
    for j in range(images):
        count = jnp.where(image == j, counts_ref[0, j], count)
        label = jnp.where(image == j, labels_ref[loss_ref[0] * images + j], label)
    count = count.astype(f32)
    embed = total / count
    norm_e = jnp.sqrt(jnp.sum(embed * embed, axis=-1, keepdims=True) + eps)
    unit_e = embed / norm_e
    wide = texts.astype(f32)
    norm_t = jnp.sqrt(jnp.sum(wide * wide, axis=-1, keepdims=True) + eps)
    inverse_t = (1.0 / norm_t).T
    scale = scale_ref[0]
    unit_parts = split_three(unit_e)
    raw = lax.dot_general(jnp.concatenate(unit_parts, axis=0), texts, NT, preferred_element_type=f32)
    raw = raw[:images] + raw[images : 2 * images] + raw[2 * images :]
    score = scale * (raw * inverse_t) + shift_ref[0]
    sign = jnp.where(iota((images, all_images), 1) == label, 1.0, -1.0)
    margin = sign * score
    dscore = -sign * jax.nn.sigmoid(-margin) / all_images
    du = jnp.dot(
        jnp.concatenate(split_three(dscore * inverse_t), axis=0), texts, preferred_element_type=f32
    )
    du = scale * (du[:images] + du[images : 2 * images] + du[2 * images :])
    dembed = (du - unit_e * jnp.sum(unit_e * du, axis=-1, keepdims=True)) / norm_e
    upstream_ref[...] = grad_scale * (dembed / count)
    high, low = split_bf16(scale * dscore)
    unit_high, unit_low = unit_parts[:2]
    parts = lax.dot_general(
        jnp.concatenate([high, high, low], axis=0),
        jnp.concatenate([unit_high, unit_low, unit_high], axis=0),
        TN,
        preferred_element_type=f32,
    )
    parts_ref[:, :width] = parts.astype(bf16)
    loss = jnp.sum(jnp.sum(log_sigmoid(margin), axis=1, keepdims=True), axis=0, keepdims=True) / -all_images
    loss_high, loss_low = split_bf16(loss)
    lane = iota((all_images, LANES), 1)
    loss_lanes = jnp.where(lane == 0, loss_high.astype(f32), jnp.where(lane == 1, loss_low.astype(f32), 0.0))
    parts_ref[:, width:] = loss_lanes.astype(bf16)


def back_kernel(
    mp_ref, upstream_ref, member_ref, slope_ref, w1t_ref, w2_ref, *refs, steps, ring
):
    outs, d_act_ref = refs[:-1], refs[-1]
    share = outs[0].shape[0]
    d_image = upstream_ref[...].astype(bf16)
    d_act = lax.dot_general(d_image, w2_ref[...], NT, preferred_element_type=f32)
    both = jnp.concatenate(split_bf16(d_act), axis=0)
    d_act_ref[...] = both
    for out_ref, step in zip(outs, steps):
        first = pl.multiple_of(lax.rem(mp_ref[0] + step, ring) * share, share)
        rows = pl.ds(first, share)
        out_ref[...] = back_rows(member_ref[rows, :], both, slope_ref[rows, :], w1t_ref[...]).astype(bf16)


def back_rows(member, both, slope, w1t):
    member = member.astype(bf16)
    d_rows = jnp.dot(jnp.concatenate([member, member], axis=1), both, preferred_element_type=f32)
    d_pre = (d_rows * slope).astype(bf16)
    return jnp.dot(d_pre, w1t, preferred_element_type=f32)


def own_kernel(d_act_ref, member_ref, slope_ref, w1t_ref, out_ref):
    out_ref[...] = back_rows(member_ref[...], d_act_ref[...], slope_ref[...], w1t_ref[...])


def row_kernel(own_ref, first_ref, second_ref, third_ref, x_ref, gain_ref, member_ref, upstream_ref, out_ref):
    back = own_ref[...] + first_ref[...].astype(f32)
    back = back + second_ref[...].astype(f32) + third_ref[...].astype(f32)
    xhat, inverse_deviation = layer_statistics(x_ref[...].astype(f32))
    dxhat = back * gain_ref[...][None, :]
    dx = inverse_deviation * (
        dxhat
        - jnp.mean(dxhat, axis=-1, keepdims=True)
        - xhat * jnp.mean(dxhat * xhat, axis=-1, keepdims=True)
    )
    upstream = jnp.dot(member_ref[...], upstream_ref[...], precision=HIGHEST, preferred_element_type=f32)
    out_ref[...] = dx + upstream


def text_kernel(parts_ref, text_ref, grad_ref, loss_ref):
    text = text_ref[...].astype(f32)
    width = text.shape[1]
    total = parts_ref[0].astype(f32)
    for k in range(1, parts_ref.shape[0]):
        total = total + parts_ref[k].astype(f32)
    norm = jnp.sqrt(jnp.sum(text * text, axis=-1, keepdims=True) + eps)
    unit = text / norm
    dv = total[:, :width]
    grad_ref[...] = (dv - unit * jnp.sum(unit * dv, axis=-1, keepdims=True)) / norm
    loss_ref[...] = jnp.sum(total[:1, width:], axis=1, keepdims=True)


def call(kernel, outs, specs, operands, flops=0, read=0):
    return pl.pallas_call(
        kernel,
        out_shape=outs,
        in_specs=specs,
        out_specs=jax.tree.map(lambda _: whole, outs),
        compiler_params=pltpu.CompilerParams(vmem_limit_bytes=VMEM_LIMIT),
        cost_estimate=pl.CostEstimate(flops=flops, bytes_accessed=read, transcendentals=0),
    )(*operands)


def shape(dims, kind):
    return jax.ShapeDtypeStruct(dims, kind)


def exchange(block, axis):
    return lax.all_to_all(block, axis, split_axis=0, concat_axis=0, tiled=True)


def shards(
    patches,
    layer_norm_gain,
    layer_norm_bias,
    fc1_weight,
    fc1_bias,
    fc2_weight,
    counts,
    owners,
    text_embed,
    labels,
    logit_scale,
    logit_bias,
):
    dp_size = lax.axis_size("dp")
    mp_size = lax.axis_size("mp")
    loss_size = lax.axis_size("loss")
    dp_index = lax.axis_index("dp").astype(jnp.int32)[None]
    mp_index = lax.axis_index("mp").astype(jnp.int32)[None]
    loss_index = lax.axis_index("loss").astype(jnp.int32)[None]
    row_count, width = patches.shape
    hidden = fc1_weight.shape[1]
    share_rows = row_count // mp_size
    images = counts.shape[1]
    all_images = labels.shape[0]
    padded = -(-row_count // dp_size // 8) * 8
    fc1_t = fc1_weight.T
    plan = owners[0]
    matmul = 2 * row_count * width * hidden
    weight_bytes = 2 * width * hidden

    outgoing, text_copies = call(
        functools.partial(pack_kernel, padded=padded),
        (shape((dp_size * padded, width), bf16), shape((all_images, width), bf16)),
        [scalars, scalars, whole, whole],
        (dp_index, plan, patches, text_embed),
    )
    incoming = exchange(outgoing, "dp")
    texts = exchange(text_copies, "loss")

    patches, outgoing = lax.optimization_barrier((patches, outgoing))
    partial_sums = call(
        functools.partial(pool_kernel, share=1.0 / mp_size),
        shape((images, width), f32),
        [scalars, scalars] + [whole] * 6,
        (dp_index, counts, patches, layer_norm_gain, layer_norm_bias, fc1_t, fc1_bias, fc2_weight),
        flops=matmul,
        read=2 * weight_bytes,
    )
    slab_sums = jnp.sum(lax.all_gather(partial_sums, "mp", axis=0), axis=0)
    slope, rows, member = call(
        slope_kernel,
        (shape((row_count, hidden), f32), shape((row_count, width), bf16), shape((row_count, images), f32)),
        [scalars, scalars] + [whole] * 6,
        (dp_index, counts, plan, incoming, layer_norm_gain, layer_norm_bias, fc1_t, fc1_bias),
        flops=matmul,
        read=2 * weight_bytes,
    )
    slab_sums, slope = lax.optimization_barrier((slab_sums, slope))
    pieces = lax.all_gather(slab_sums, "dp", axis=0)
    upstream, parts = call(
        embed_kernel,
        (shape((images, width), f32), shape((all_images, width + LANES), bf16)),
        [scalars] * 5 + [whole] * 2,
        (loss_index, counts, labels, logit_scale, logit_bias, pieces, texts),
    )
    steps = (2, 1, 3)
    *remote, d_act = call(
        functools.partial(back_kernel, steps=steps, ring=mp_size),
        [shape((share_rows, width), bf16)] * len(steps) + [shape((2 * images, hidden), bf16)],
        [scalars] + [whole] * 5,
        (mp_index, upstream, member, slope, fc1_t, fc2_weight),
        flops=matmul,
        read=2 * weight_bytes,
    )
    received = []
    for chunk, step in zip(remote, steps):
        pairs = [(i, (i + step) % mp_size) for i in range(mp_size)]
        received.append(lax.ppermute(chunk, "mp", pairs))
    first_row = mp_index[0] * share_rows
    own_rows = lax.dynamic_slice_in_dim(rows, first_row, share_rows, 0)
    own_member = lax.dynamic_slice_in_dim(member, first_row, share_rows, 0)
    own_slope = lax.dynamic_slice_in_dim(slope, first_row, share_rows, 0)
    own_back = call(
        own_kernel,
        shape((share_rows, width), f32),
        [whole] * 4,
        (d_act, own_member, own_slope, fc1_t),
        flops=matmul // mp_size,
        read=weight_bytes,
    )
    all_parts = exchange(parts, "loss").reshape(loss_size, images, width + LANES)
    grad_text, loss = call(
        text_kernel,
        (shape((images, width), f32), shape((1, 1), f32)),
        [whole] * 2,
        (all_parts, text_embed),
    )
    grad_rows = call(
        row_kernel,
        shape((share_rows, width), f32),
        [whole] * 8,
        (own_back, *received, own_rows, layer_norm_gain, own_member, upstream),
    )
    return (grad_rows, grad_text, loss[0, 0])


def solution(mesh):
    placed = (
        P(("dp", "loss"), None),
        P(),
        P(),
        P(None, "mp"),
        P("mp"),
        P("mp", None),
        P("loss", None),
        P("loss", None, None),
        P("loss", None),
        P(),
        P(),
        P(),
    )
    return jax.shard_map(
        shards,
        mesh=mesh,
        in_specs=placed,
        out_specs=(P(("dp", "loss", "mp"), None), P("loss", None), P()),
        check_vma=False,
    )
```

```python
import functools

import jax
import jax.numpy as jnp
from jax import lax
from jax.experimental import pallas as pl
from jax.experimental.pallas import tpu as pltpu
from jax.sharding import PartitionSpec as P

eps = 1e-06
grad_scale = 262144.0
gelu_coef = 0.7978845608028654
f32 = jnp.float32
bf16 = jnp.bfloat16
VMEM_LIMIT = 28 * 1024 * 1024
whole = pl.BlockSpec(memory_space=pltpu.VMEM)
scalars = pl.BlockSpec(memory_space=pltpu.SMEM)
stored = pl.BlockSpec(memory_space=pltpu.HBM)
NT = (((1,), (1,)), ((), ()))
TN = (((0,), (0,)), ((), ()))
LANES = 128
HIGHEST = lax.Precision.HIGHEST


def column_chunks(width, step):
    return [(first, min(step, width - first)) for first in range(0, width, step)]


def layer_statistics(floats):
    center = floats - jnp.mean(floats, axis=-1, keepdims=True)
    spread = jnp.mean(center * center, axis=-1, keepdims=True)
    inverse_deviation = lax.rsqrt(spread + eps)
    return center * inverse_deviation, inverse_deviation


def split_bf16(values):
    high = values.astype(bf16)
    return high, (values - high.astype(f32)).astype(bf16)


def fetch(sources, targets, semaphores):
    copies = [
        pltpu.make_async_copy(source, target, semaphores.at[k])
        for k, (source, target) in enumerate(zip(sources, targets))
    ]
    for copy in copies:
        copy.start()
    return copies


def split_three(values):
    high, rest = split_bf16(values)
    return high, rest, (values - high.astype(f32) - rest.astype(f32)).astype(bf16)


def quotient(values, by):
    return (values * (65536 // by + 1)) >> 16


def iota(dims, axis):
    return lax.broadcasted_iota(jnp.int32, dims, axis)


def one_hot(condition):
    return jnp.where(condition, 1.0, 0.0).astype(bf16)


def pack_kernel(dp_ref, owners_hbm, x_hbm, out_ref, owners_ref, x_ref, semaphores, *, padded):
    copies = fetch((owners_hbm.at[0], x_hbm), (owners_ref, x_ref), semaphores)
    rows = x_ref.shape[0]
    slots = owners_ref.shape[0]
    block_rows = rows // slots
    block = quotient(iota((1, rows), 1), block_rows)
    within = iota((1, rows), 1) - block * block_rows
    owner = jnp.zeros((1, rows), jnp.int32)
    copies[0].wait()
    for b in range(slots):
        owner = jnp.where(block == b, owners_ref[dp_ref[0], b], owner)
    target = owner * padded + within
    pick = one_hot(iota((slots * padded, rows), 0) == target)
    copies[1].wait()
    out_ref[...] = jnp.dot(pick, x_ref[...], preferred_element_type=f32).astype(bf16)


def image_bounds(counts_ref, dims, axis):
    image = iota(dims, axis)
    starts = jnp.zeros(dims, jnp.int32)
    ends = jnp.zeros(dims, jnp.int32)
    first = jnp.int32(0)
    for j in range(counts_ref.shape[1]):
        last = first + counts_ref[0, j]
        starts = jnp.where(image == j, first, starts)
        ends = jnp.where(image == j, last, ends)
        first = last
    return starts, ends


def pool_kernel(
    dp_ref,
    counts_hbm,
    x_hbm,
    gain_hbm,
    bias_hbm,
    b1_hbm,
    w1t_hbm,
    w2_hbm,
    out_ref,
    counts_ref,
    x_ref,
    gain_ref,
    bias_ref,
    b1_ref,
    w1t_ref,
    w2_ref,
    semaphores,
    *,
    share,
):
    copies = fetch(
        (counts_hbm, x_hbm, gain_hbm, bias_hbm, b1_hbm, w1t_hbm, w2_hbm),
        (counts_ref, x_ref, gain_ref, bias_ref, b1_ref, w1t_ref, w2_ref),
        semaphores,
    )
    for copy in copies[:5]:
        copy.wait()
    rows = x_ref.shape[0]
    images = counts_ref.shape[1]
    position = dp_ref[0] * rows + iota((images, rows), 1)
    starts, ends = image_bounds(counts_ref, (images, 1), 0)
    member = one_hot((position >= starts) & (position < ends))
    x = x_ref[...]
    xhat, _ = layer_statistics(x.astype(f32))
    normed = (xhat * gain_ref[...][None, :] + bias_ref[...][None, :]).astype(bf16)
    offset = b1_ref[...][None, :]
    total = share * jnp.dot(member, x, preferred_element_type=f32)
    for copy in copies[5:]:
        copy.wait()
    for first, many in column_chunks(w1t_ref.shape[0], 256):
        cols = slice(first, first + many)
        pre = lax.dot_general(normed, w1t_ref[cols, :], NT, preferred_element_type=f32) + offset[:, cols]
        inner = gelu_coef * (pre + 0.044715 * pre * pre * pre)
        act = (0.5 * pre * (1.0 + jnp.tanh(inner))).astype(bf16)
        pooled = jnp.dot(member, act, preferred_element_type=f32)
        both = jnp.concatenate(split_bf16(pooled), axis=0)
        product = jnp.dot(both, w2_ref[cols, :], preferred_element_type=f32)
        total = total + product[:images] + product[images:]
    out_ref[...] = total


def slope_kernel(
    dp_ref,
    in_ref,
    counts_hbm,
    owners_hbm,
    gain_hbm,
    bias_hbm,
    b1_hbm,
    text_hbm,
    w1t_hbm,
    slope_ref,
    rows_ref,
    member_ref,
    texts_ref,
    counts_ref,
    owners_ref,
    gain_ref,
    bias_ref,
    b1_ref,
    text_ref,
    w1t_ref,
    semaphores,
):
    copies = fetch(
        (counts_hbm, owners_hbm.at[0], gain_hbm, bias_hbm, b1_hbm, text_hbm, w1t_hbm),
        (counts_ref, owners_ref, gain_ref, bias_ref, b1_ref, text_ref, w1t_ref),
        semaphores,
    )
    rows = rows_ref.shape[0]
    slots = owners_ref.shape[0]
    block_rows = rows // slots
    padded = in_ref.shape[0] // slots
    source = quotient(iota((rows, 1), 0), block_rows)
    within = iota((rows, 1), 0) - source * block_rows
    pick = one_hot(iota((rows, in_ref.shape[0]), 1) == source * padded + within)
    x = jnp.dot(pick, in_ref[...], preferred_element_type=f32)
    rows_ref[...] = x.astype(bf16)
    for copy in copies[:6]:
        copy.wait()
    text = text_ref[...].astype(f32)
    texts_ref[...] = jnp.concatenate([text] * (texts_ref.shape[0] // text.shape[0]), axis=0).astype(bf16)
    block = jnp.where(owners_ref[...] == dp_ref[0], iota((slots, slots), 1), 0)
    block = jnp.sum(block.astype(f32), axis=1, keepdims=True)
    by_source = one_hot(iota((rows, slots), 1) == source)
    block = jnp.dot(by_source, jnp.broadcast_to(block, (slots, LANES)).astype(bf16), preferred_element_type=f32)
    position = source * rows + block[:, :1].astype(jnp.int32) * block_rows + within
    starts, ends = image_bounds(counts_ref, (1, member_ref.shape[1]), 1)
    member_ref[...] = jnp.where((position >= starts) & (position < ends), 1.0, 0.0)
    xhat, _ = layer_statistics(x)
    normed = (xhat * gain_ref[...][None, :] + bias_ref[...][None, :]).astype(bf16)
    offset = b1_ref[...][None, :]
    copies[6].wait()
    for first, many in column_chunks(w1t_ref.shape[0], 256):
        cols = slice(first, first + many)
        pre = lax.dot_general(normed, w1t_ref[cols, :], NT, preferred_element_type=f32) + offset[:, cols]
        square = pre * pre
        tanh_part = jnp.tanh(gelu_coef * (pre + 0.044715 * square * pre))
        slope_ref[:, cols] = 0.5 * (1.0 + tanh_part) + 0.5 * pre * (
            1.0 - tanh_part * tanh_part
        ) * gelu_coef * (1.0 + 0.134145 * square)


def log_sigmoid(values):
    return jnp.minimum(values, 0.0) - jnp.log1p(jnp.exp(-jnp.abs(values)))


def gradient_kernel(
    loss_ref,
    mp_ref,
    scale_ref,
    shift_ref,
    pieces_ref,
    texts_ref,
    member_ref,
    slope_ref,
    counts_hbm,
    labels_hbm,
    w2_hbm,
    w1t_hbm,
    upstream_ref,
    parts_ref,
    d_act_ref,
    *refs,
    steps,
    ring,
):
    outs, (counts_ref, labels_ref, w2_ref, w1t_ref, semaphores) = refs[: len(steps)], refs[len(steps) :]
    copies = fetch(
        (counts_hbm, labels_hbm, w2_hbm, w1t_hbm), (counts_ref, labels_ref, w2_ref, w1t_ref), semaphores
    )
    total = pieces_ref[0]
    for k in range(1, pieces_ref.shape[0]):
        total = total + pieces_ref[k]
    images, width = total.shape
    copies[0].wait()
    copies[1].wait()
    texts = texts_ref[...]
    all_images = texts.shape[0]
    image = iota((images, 1), 0)
    count = jnp.zeros((images, 1), jnp.int32)
    label = jnp.zeros((images, 1), jnp.int32)
    for j in range(images):
        count = jnp.where(image == j, counts_ref[0, j], count)
        label = jnp.where(image == j, labels_ref[loss_ref[0] * images + j], label)
    count = count.astype(f32)
    embed = total / count
    norm_e = jnp.sqrt(jnp.sum(embed * embed, axis=-1, keepdims=True) + eps)
    unit_e = embed / norm_e
    wide = texts.astype(f32)
    norm_t = jnp.sqrt(jnp.sum(wide * wide, axis=-1, keepdims=True) + eps)
    inverse_t = (1.0 / norm_t).T
    scale = scale_ref[0]
    unit_parts = split_three(unit_e)
    raw = lax.dot_general(jnp.concatenate(unit_parts, axis=0), texts, NT, preferred_element_type=f32)
    raw = raw[:images] + raw[images : 2 * images] + raw[2 * images :]
    score = scale * (raw * inverse_t) + shift_ref[0]
    sign = jnp.where(iota((images, all_images), 1) == label, 1.0, -1.0)
    margin = sign * score
    dscore = -sign * jax.nn.sigmoid(-margin) / all_images
    du = jnp.dot(
        jnp.concatenate(split_three(dscore * inverse_t), axis=0), texts, preferred_element_type=f32
    )
    du = scale * (du[:images] + du[images : 2 * images] + du[2 * images :])
    dembed = (du - unit_e * jnp.sum(unit_e * du, axis=-1, keepdims=True)) / norm_e
    upstream_ref[...] = grad_scale * (dembed / count)
    high, low = split_bf16(scale * dscore)
    unit_high, unit_low = unit_parts[:2]
    parts = lax.dot_general(
        jnp.concatenate([high, high, low], axis=0),
        jnp.concatenate([unit_high, unit_low, unit_high], axis=0),
        TN,
        preferred_element_type=f32,
    )
    parts_ref[:, :width] = parts.astype(bf16)
    loss = jnp.sum(jnp.sum(log_sigmoid(margin), axis=1, keepdims=True), axis=0, keepdims=True) / -all_images
    loss_high, loss_low = split_bf16(loss)
    lane = iota((all_images, LANES), 1)
    loss_lanes = jnp.where(lane == 0, loss_high.astype(f32), jnp.where(lane == 1, loss_low.astype(f32), 0.0))
    parts_ref[:, width:] = loss_lanes.astype(bf16)
    copies[2].wait()
    d_image = upstream_ref[...].astype(bf16)
    d_act = lax.dot_general(d_image, w2_ref[...], NT, preferred_element_type=f32)
    both = jnp.concatenate(split_bf16(d_act), axis=0)
    d_act_ref[...] = both
    copies[3].wait()
    share = outs[0].shape[0]
    for out_ref, step in zip(outs, steps):
        rows = own_range(mp_ref, step, ring, share)
        out_ref[...] = back_rows(member_ref[rows, :], both, slope_ref[rows, :], w1t_ref[...]).astype(bf16)


def own_range(mp_ref, step, ring, share):
    return pl.ds(pl.multiple_of(lax.rem(mp_ref[0] + step, ring) * share, share), share)


def back_rows(member, both, slope, w1t):
    member = member.astype(bf16)
    d_rows = jnp.dot(jnp.concatenate([member, member], axis=1), both, preferred_element_type=f32)
    d_pre = (d_rows * slope).astype(bf16)
    return jnp.dot(d_pre, w1t, preferred_element_type=f32)


def own_kernel(mp_ref, d_act_ref, member_ref, slope_ref, w1t_hbm, out_ref, w1t_ref, semaphores, *, ring):
    copies = fetch((w1t_hbm,), (w1t_ref,), semaphores)
    rows = own_range(mp_ref, 0, ring, out_ref.shape[0])
    copies[0].wait()
    out_ref[...] = back_rows(member_ref[rows, :], d_act_ref[...], slope_ref[rows, :], w1t_ref[...])


def row_kernel(
    mp_ref,
    own_ref,
    first_ref,
    second_ref,
    third_ref,
    x_ref,
    member_ref,
    upstream_ref,
    gain_hbm,
    out_ref,
    gain_ref,
    semaphores,
    *,
    ring,
):
    copies = fetch((gain_hbm,), (gain_ref,), semaphores)
    rows = own_range(mp_ref, 0, ring, out_ref.shape[0])
    back = own_ref[...] + first_ref[...].astype(f32)
    back = back + second_ref[...].astype(f32) + third_ref[...].astype(f32)
    xhat, inverse_deviation = layer_statistics(x_ref[rows, :].astype(f32))
    copies[0].wait()
    dxhat = back * gain_ref[...][None, :]
    dx = inverse_deviation * (
        dxhat
        - jnp.mean(dxhat, axis=-1, keepdims=True)
        - xhat * jnp.mean(dxhat * xhat, axis=-1, keepdims=True)
    )
    upstream = jnp.dot(member_ref[rows, :], upstream_ref[...], precision=HIGHEST, preferred_element_type=f32)
    out_ref[...] = dx + upstream


def text_kernel(parts_ref, text_ref, grad_ref, loss_ref):
    text = text_ref[...].astype(f32)
    width = text.shape[1]
    total = parts_ref[0].astype(f32)
    for k in range(1, parts_ref.shape[0]):
        total = total + parts_ref[k].astype(f32)
    norm = jnp.sqrt(jnp.sum(text * text, axis=-1, keepdims=True) + eps)
    unit = text / norm
    dv = total[:, :width]
    grad_ref[...] = (dv - unit * jnp.sum(unit * dv, axis=-1, keepdims=True)) / norm
    loss_ref[...] = jnp.sum(total[:1, width:], axis=1, keepdims=True)


def call(kernel, outs, operands, scratch=(), flops=0, read=0):
    fetched = sum(space is stored for space, _ in operands)
    extra = [pltpu.SemaphoreType.DMA((fetched,))] if fetched else []
    return pl.pallas_call(
        kernel,
        out_shape=outs,
        in_specs=[space for space, _ in operands],
        out_specs=jax.tree.map(lambda _: whole, outs),
        scratch_shapes=list(scratch) + extra,
        compiler_params=pltpu.CompilerParams(vmem_limit_bytes=VMEM_LIMIT),
        cost_estimate=pl.CostEstimate(flops=flops, bytes_accessed=read, transcendentals=0),
    )(*[pltpu.with_memory_space_constraint(array, pltpu.HBM) if space is stored else array for space, array in operands])


def shape(dims, kind):
    return jax.ShapeDtypeStruct(dims, kind)


def exchange(block, axis):
    return lax.all_to_all(block, axis, split_axis=0, concat_axis=0, tiled=True)


def shards(
    patches,
    layer_norm_gain,
    layer_norm_bias,
    fc1_weight,
    fc1_bias,
    fc2_weight,
    counts,
    owners,
    text_embed,
    labels,
    logit_scale,
    logit_bias,
):
    dp_size = lax.axis_size("dp")
    mp_size = lax.axis_size("mp")
    loss_size = lax.axis_size("loss")
    dp_index = lax.axis_index("dp").astype(jnp.int32)[None]
    mp_index = lax.axis_index("mp").astype(jnp.int32)[None]
    loss_index = lax.axis_index("loss").astype(jnp.int32)[None]
    row_count, width = patches.shape
    hidden = fc1_weight.shape[1]
    share_rows = row_count // mp_size
    images = counts.shape[1]
    all_images = labels.shape[0]
    padded = -(-row_count // dp_size // 8) * 8
    fc1_t = fc1_weight.T
    matmul = 2 * row_count * width * hidden
    weight_bytes = 2 * width * hidden

    gain, bias, offset = layer_norm_gain, layer_norm_bias, fc1_bias
    gain_room, offset_room = pltpu.VMEM((width,), f32), pltpu.VMEM((hidden,), f32)
    plan_dims, counts_dims = owners.shape[1:], counts.shape
    first_room, second_room = pltpu.VMEM((hidden, width), bf16), pltpu.VMEM((hidden, width), bf16)

    outgoing = call(
        functools.partial(pack_kernel, padded=padded),
        shape((dp_size * padded, width), bf16),
        [(scalars, dp_index), (stored, owners), (stored, patches)],
        [pltpu.SMEM(plan_dims, jnp.int32), pltpu.VMEM((row_count, width), bf16)],
    )
    incoming = exchange(outgoing, "dp")

    patches, outgoing = lax.optimization_barrier((patches, outgoing))
    partial_sums = call(
        functools.partial(pool_kernel, share=1.0 / mp_size),
        shape((images, width), f32),
        [(scalars, dp_index)]
        + [(stored, array) for array in (counts, patches, gain, bias, offset, fc1_t, fc2_weight)],
        [
            pltpu.SMEM(counts_dims, jnp.int32),
            pltpu.VMEM((row_count, width), bf16),
            gain_room,
            gain_room,
            offset_room,
            first_room,
            second_room,
        ],
        flops=matmul,
        read=2 * weight_bytes,
    )
    slab_sums = jnp.sum(lax.all_gather(partial_sums, "mp", axis=0), axis=0)
    incoming, slab_sums = lax.optimization_barrier((incoming, slab_sums))
    slope, rows, member, text_copies = call(
        slope_kernel,
        (
            shape((row_count, hidden), f32),
            shape((row_count, width), bf16),
            shape((row_count, images), f32),
            shape((all_images, width), bf16),
        ),
        [(scalars, dp_index), (whole, incoming)]
        + [(stored, array) for array in (counts, owners, gain, bias, offset, text_embed, fc1_t)],
        [
            pltpu.SMEM(counts_dims, jnp.int32),
            pltpu.VMEM(plan_dims, jnp.int32),
            gain_room,
            gain_room,
            offset_room,
            pltpu.VMEM((images, width), bf16),
            first_room,
        ],
        flops=matmul,
        read=2 * weight_bytes,
    )
    texts = exchange(text_copies, "loss")
    slab_sums, slope = lax.optimization_barrier((slab_sums, slope))
    pieces = lax.all_gather(slab_sums, "dp", axis=0)
    steps = (2, 1, 3)
    upstream, parts, d_act, *chunks = call(
        functools.partial(gradient_kernel, steps=steps, ring=mp_size),
        [
            shape((images, width), f32),
            shape((all_images, width + LANES), bf16),
            shape((2 * images, hidden), bf16),
        ]
        + [shape((share_rows, width), bf16)] * len(steps),
        [(scalars, array) for array in (loss_index, mp_index, logit_scale, logit_bias)]
        + [(whole, array) for array in (pieces, texts, member, slope)]
        + [(stored, array) for array in (counts, labels, fc2_weight, fc1_t)],
        [
            pltpu.SMEM(counts_dims, jnp.int32),
            pltpu.SMEM((all_images,), jnp.int32),
            second_room,
            first_room,
        ],
        flops=matmul,
        read=2 * weight_bytes,
    )
    received = []
    for chunk, step in zip(chunks, steps):
        pairs = [(i, (i + step) % mp_size) for i in range(mp_size)]
        received.append(lax.ppermute(chunk, "mp", pairs))
    own_back = call(
        functools.partial(own_kernel, ring=mp_size),
        shape((share_rows, width), f32),
        [(scalars, mp_index), (whole, d_act), (whole, member), (whole, slope), (stored, fc1_t)],
        [first_room],
        flops=matmul // mp_size,
        read=weight_bytes,
    )
    parts, own_back = lax.optimization_barrier((parts, own_back))
    all_parts = exchange(parts, "loss").reshape(loss_size, images, width + LANES)
    grad_text, loss = call(
        text_kernel,
        (shape((images, width), f32), shape((1, 1), f32)),
        [(whole, all_parts), (whole, text_embed)],
    )
    grad_rows = call(
        functools.partial(row_kernel, ring=mp_size),
        shape((share_rows, width), f32),
        [(scalars, mp_index), (whole, own_back)]
        + [(whole, array) for array in received]
        + [(whole, rows), (whole, member), (whole, upstream), (stored, gain)],
        [gain_room],
    )
    return (grad_rows, grad_text, loss[0, 0])


def solution(mesh):
    placed = (
        P(("dp", "loss"), None),
        P(),
        P(),
        P(None, "mp"),
        P("mp"),
        P("mp", None),
        P("loss", None),
        P("loss", None, None),
        P("loss", None),
        P(),
        P(),
        P(),
    )
    return jax.shard_map(
        shards,
        mesh=mesh,
        in_specs=placed,
        out_specs=(P(("dp", "loss", "mp"), None), P("loss", None), P()),
        check_vma=False,
    )
```

```python
import functools

import jax
import jax.numpy as jnp
from jax import lax
from jax.experimental import pallas as pl
from jax.experimental.pallas import tpu as pltpu
from jax.sharding import PartitionSpec as P

eps = 1e-06
grad_scale = 262144.0
gelu_coef = 0.7978845608028654
f32 = jnp.float32
bf16 = jnp.bfloat16
VMEM_LIMIT = 28 * 1024 * 1024
whole = pl.BlockSpec(memory_space=pltpu.VMEM)
scalars = pl.BlockSpec(memory_space=pltpu.SMEM)
stored = pl.BlockSpec(memory_space=pltpu.HBM)
NT = (((1,), (1,)), ((), ()))
TN = (((0,), (0,)), ((), ()))
LANES = 128
HIDDEN_STEP = 256
COPY_STEP = 384
MOST_COPIES = 24
HIGHEST = lax.Precision.HIGHEST


def column_chunks(width, step):
    return [(first, min(step, width - first)) for first in range(0, width, step)]


def layer_statistics(floats):
    center = floats - jnp.mean(floats, axis=-1, keepdims=True)
    spread = jnp.mean(center * center, axis=-1, keepdims=True)
    inverse_deviation = lax.rsqrt(spread + eps)
    return center * inverse_deviation, inverse_deviation


def stacked_parts(values, many):
    parts = []
    for _ in range(many):
        part = values.astype(bf16).astype(f32)
        parts.append(part)
        values = values - part
    return jnp.concatenate(parts, axis=0).astype(bf16)


def fetch(sources, targets, semaphores, first=0):
    copies = [
        pltpu.make_async_copy(source, target, semaphores.at[first + k])
        for k, (source, target) in enumerate(zip(sources, targets))
    ]
    for copy in copies:
        copy.start()
    return copies


def row_pieces(array, step):
    return [array.at[pl.ds(first, many), :] for first, many in column_chunks(array.shape[0], step)]


def column_pieces(array, step):
    return [array.at[:, pl.ds(first, many)] for first, many in column_chunks(array.shape[1], step)]


def wait_all(copies):
    for copy in copies:
        copy.wait()


def quotient(values, by):
    return (values * (65536 // by + 1)) >> 16


def iota(dims, axis):
    return lax.broadcasted_iota(jnp.int32, dims, axis)


def one_hot(condition):
    return jnp.where(condition, 1.0, 0.0).astype(bf16)


def pack_kernel(dp_ref, owners_hbm, x_hbm, out_ref, owners_ref, x_ref, semaphores, *, padded):
    copies = fetch((owners_hbm.at[0],), (owners_ref,), semaphores)
    copies += fetch(row_pieces(x_hbm, 80), row_pieces(x_ref, 80), semaphores, 1)
    rows = x_ref.shape[0]
    slots = owners_ref.shape[0]
    block_rows = rows // slots
    block = quotient(iota((1, rows), 1), block_rows)
    within = iota((1, rows), 1) - block * block_rows
    owner = jnp.zeros((1, rows), jnp.int32)
    copies[0].wait()
    for b in range(slots):
        owner = jnp.where(block == b, owners_ref[dp_ref[0], b], owner)
    target = owner * padded + within
    pick = one_hot(iota((slots * padded, rows), 0) == target)
    wait_all(copies[1:])
    out_ref[...] = jnp.dot(pick, x_ref[...], preferred_element_type=f32).astype(bf16)


def image_bounds(counts_ref, dims, axis):
    image = iota(dims, axis)
    starts = jnp.zeros(dims, jnp.int32)
    ends = jnp.zeros(dims, jnp.int32)
    first = jnp.int32(0)
    for j in range(counts_ref.shape[1]):
        last = first + counts_ref[0, j]
        starts = jnp.where(image == j, first, starts)
        ends = jnp.where(image == j, last, ends)
        first = last
    return starts, ends


def pool_kernel(
    dp_ref,
    counts_hbm,
    x_hbm,
    gain_hbm,
    bias_hbm,
    b1_hbm,
    w1t_hbm,
    w2_hbm,
    out_ref,
    counts_ref,
    x_ref,
    gain_ref,
    bias_ref,
    b1_ref,
    w1t_ref,
    w2_ref,
    semaphores,
    *,
    share,
):
    copies = fetch(
        (counts_hbm, gain_hbm, bias_hbm, b1_hbm, *row_pieces(x_hbm, 80)),
        (counts_ref, gain_ref, bias_ref, b1_ref, *row_pieces(x_ref, 80)),
        semaphores,
    )
    begin = len(copies)
    firsts = fetch(column_pieces(w1t_hbm, COPY_STEP), column_pieces(w1t_ref, COPY_STEP), semaphores, begin)
    begin += len(firsts)
    seconds = fetch(column_pieces(w2_hbm, COPY_STEP), column_pieces(w2_ref, COPY_STEP), semaphores, begin)
    wait_all(copies)
    rows = x_ref.shape[0]
    images = counts_ref.shape[1]
    position = dp_ref[0] * rows + iota((images, rows), 1)
    starts, ends = image_bounds(counts_ref, (images, 1), 0)
    member = one_hot((position >= starts) & (position < ends))
    x = x_ref[...]
    xhat, _ = layer_statistics(x.astype(f32))
    normed = (xhat * gain_ref[...][None, :] + bias_ref[...][None, :]).astype(bf16)
    offset = b1_ref[...][None, :]
    total = share * jnp.dot(member, x, preferred_element_type=f32)
    wait_all(firsts)
    for first, many in column_chunks(w1t_ref.shape[0], HIDDEN_STEP):
        cols = slice(first, first + many)
        pre = lax.dot_general(normed, w1t_ref[cols, :], NT, preferred_element_type=f32) + offset[:, cols]
        inner = gelu_coef * (pre + 0.044715 * pre * pre * pre)
        act = (0.5 * pre * (1.0 + jnp.tanh(inner))).astype(bf16)
        pooled = jnp.dot(member, act, preferred_element_type=f32)
        if first == 0:
            wait_all(seconds)
        both = stacked_parts(pooled, 2)
        product = jnp.dot(both, w2_ref[cols, :], preferred_element_type=f32)
        total = total + product[:images] + product[images:]
    out_ref[...] = total


def slope_kernel(
    dp_ref,
    in_ref,
    counts_hbm,
    owners_hbm,
    gain_hbm,
    bias_hbm,
    b1_hbm,
    text_hbm,
    w1t_hbm,
    slope_ref,
    rows_ref,
    member_ref,
    texts_ref,
    counts_ref,
    owners_ref,
    gain_ref,
    bias_ref,
    b1_ref,
    text_ref,
    w1t_ref,
    semaphores,
):
    copies = fetch(
        (counts_hbm, owners_hbm.at[0], gain_hbm, bias_hbm, b1_hbm, text_hbm),
        (counts_ref, owners_ref, gain_ref, bias_ref, b1_ref, text_ref),
        semaphores,
    )
    firsts = fetch(column_pieces(w1t_hbm, COPY_STEP), column_pieces(w1t_ref, COPY_STEP), semaphores, len(copies))
    rows = rows_ref.shape[0]
    slots = owners_ref.shape[0]
    block_rows = rows // slots
    padded = in_ref.shape[0] // slots
    source = quotient(iota((rows, 1), 0), block_rows)
    within = iota((rows, 1), 0) - source * block_rows
    pick = one_hot(iota((rows, in_ref.shape[0]), 1) == source * padded + within)
    x = jnp.dot(pick, in_ref[...], preferred_element_type=f32)
    rows_ref[...] = x.astype(bf16)
    wait_all(copies)
    text = text_ref[...].astype(f32)
    texts_ref[...] = jnp.concatenate([text] * (texts_ref.shape[0] // text.shape[0]), axis=0).astype(bf16)
    block = jnp.where(owners_ref[...] == dp_ref[0], iota((slots, slots), 1), 0)
    block = jnp.sum(block.astype(f32), axis=1, keepdims=True)
    by_source = one_hot(iota((rows, slots), 1) == source)
    block = jnp.dot(by_source, jnp.broadcast_to(block, (slots, LANES)).astype(bf16), preferred_element_type=f32)
    position = source * rows + block[:, :1].astype(jnp.int32) * block_rows + within
    starts, ends = image_bounds(counts_ref, (1, member_ref.shape[1]), 1)
    member_ref[...] = jnp.where((position >= starts) & (position < ends), 1.0, 0.0)
    xhat, _ = layer_statistics(x)
    normed = (xhat * gain_ref[...][None, :] + bias_ref[...][None, :]).astype(bf16)
    offset = b1_ref[...][None, :]
    wait_all(firsts)
    for first, many in column_chunks(w1t_ref.shape[0], HIDDEN_STEP):
        cols = slice(first, first + many)
        pre = lax.dot_general(normed, w1t_ref[cols, :], NT, preferred_element_type=f32) + offset[:, cols]
        square = pre * pre
        tanh_part = jnp.tanh(gelu_coef * (pre + 0.044715 * square * pre))
        slope_ref[:, cols] = 0.5 * (1.0 + tanh_part) + 0.5 * pre * (
            1.0 - tanh_part * tanh_part
        ) * gelu_coef * (1.0 + 0.134145 * square)


def log_sigmoid(values):
    return jnp.minimum(values, 0.0) - jnp.log1p(jnp.exp(-jnp.abs(values)))


def gradient_kernel(
    loss_ref,
    mp_ref,
    scale_ref,
    shift_ref,
    pieces_ref,
    texts_ref,
    member_ref,
    slope_ref,
    counts_hbm,
    labels_hbm,
    w2_hbm,
    w1t_hbm,
    upstream_ref,
    parts_ref,
    d_act_ref,
    out_ref,
    counts_ref,
    labels_ref,
    w2_ref,
    w1t_ref,
    semaphores,
    *,
    ring,
):
    copies = fetch((counts_hbm, labels_hbm), (counts_ref, labels_ref), semaphores)
    begin = len(copies)
    seconds = fetch(column_pieces(w2_hbm, COPY_STEP), column_pieces(w2_ref, COPY_STEP), semaphores, begin)
    begin += len(seconds)
    firsts = fetch(column_pieces(w1t_hbm, COPY_STEP), column_pieces(w1t_ref, COPY_STEP), semaphores, begin)
    total = pieces_ref[0]
    for k in range(1, pieces_ref.shape[0]):
        total = total + pieces_ref[k]
    images, width = total.shape
    wait_all(copies)
    texts = texts_ref[...]
    all_images = texts.shape[0]
    image = iota((images, 1), 0)
    count = jnp.zeros((images, 1), jnp.int32)
    label = jnp.zeros((images, 1), jnp.int32)
    for j in range(images):
        count = jnp.where(image == j, counts_ref[0, j], count)
        label = jnp.where(image == j, labels_ref[loss_ref[0] * images + j], label)
    count = count.astype(f32)
    embed = total / count
    norm_e = jnp.sqrt(jnp.sum(embed * embed, axis=-1, keepdims=True) + eps)
    unit_e = embed / norm_e
    wide = texts.astype(f32)
    norm_t = jnp.sqrt(jnp.sum(wide * wide, axis=-1, keepdims=True) + eps)
    inverse_t = (1.0 / norm_t).T
    scale = scale_ref[0]
    raw = lax.dot_general(stacked_parts(unit_e, 3), texts, NT, preferred_element_type=f32)
    raw = raw[:images] + raw[images : 2 * images] + raw[2 * images :]
    score = scale * (raw * inverse_t) + shift_ref[0]
    sign = jnp.where(iota((images, all_images), 1) == label, 1.0, -1.0)
    margin = sign * score
    dscore = -sign * jax.nn.sigmoid(-margin) / all_images
    du = jnp.dot(stacked_parts(dscore * inverse_t, 3), texts, preferred_element_type=f32)
    du = scale * (du[:images] + du[images : 2 * images] + du[2 * images :])
    dembed = (du - unit_e * jnp.sum(unit_e * du, axis=-1, keepdims=True)) / norm_e
    upstream_ref[...] = grad_scale * (dembed / count)
    scaled = stacked_parts(scale * dscore, 2).astype(f32)
    unit = stacked_parts(unit_e, 2).astype(f32)
    parts = lax.dot_general(
        jnp.concatenate([scaled[:images], scaled], axis=0).astype(bf16),
        jnp.concatenate([unit, unit[:images]], axis=0).astype(bf16),
        TN,
        preferred_element_type=f32,
    )
    parts_ref[:, :width] = parts.astype(bf16)
    loss = jnp.sum(jnp.sum(log_sigmoid(margin), axis=1, keepdims=True), axis=0, keepdims=True) / -all_images
    loss_high = loss.astype(bf16).astype(f32)
    lane = iota((all_images, LANES), 1)
    loss_lanes = jnp.where(lane == 0, loss_high, jnp.where(lane == 1, loss - loss_high, 0.0))
    parts_ref[:, width:] = loss_lanes.astype(bf16)
    wait_all(seconds)
    d_image = upstream_ref[...].astype(bf16)
    d_act = lax.dot_general(d_image, w2_ref[...], NT, preferred_element_type=f32)
    both = stacked_parts(d_act, 2)
    d_act_ref[...] = both
    wait_all(firsts)
    share = out_ref.shape[0] // 2
    back = back_of_shares(mp_ref, (mp_ref[1], 2), ring, share, member_ref, both, slope_ref, w1t_ref)
    out_ref[...] = back.astype(bf16)


def share_range(mp_ref, step, ring, share):
    return pl.ds(pl.multiple_of(lax.rem(mp_ref[0] + step, ring) * share, share), share)


def back_of_shares(mp_ref, steps, ring, share, member_ref, d_act, slope_ref, w1t_ref):
    ranges = [share_range(mp_ref, step, ring, share) for step in steps]
    member = jnp.concatenate([member_ref[rows, :] for rows in ranges], axis=0)
    slope = jnp.concatenate([slope_ref[rows, :] for rows in ranges], axis=0)
    return back_rows(member, d_act, slope, w1t_ref[...])


def back_rows(member, both, slope, w1t):
    d_rows = jnp.dot(jnp.concatenate([member, member], axis=1).astype(bf16), both, preferred_element_type=f32)
    d_pre = (d_rows * slope).astype(bf16)
    return jnp.dot(d_pre, w1t, preferred_element_type=f32)


def rest_kernel(mp_ref, d_act_ref, member_ref, slope_ref, w1t_hbm, second_ref, own_ref, w1t_ref, semaphores, *, ring):
    firsts = fetch(column_pieces(w1t_hbm, COPY_STEP), column_pieces(w1t_ref, COPY_STEP), semaphores)
    wait_all(firsts)
    share = own_ref.shape[0]
    steps = (ring - mp_ref[1], 0)
    back = back_of_shares(mp_ref, steps, ring, share, member_ref, d_act_ref[...], slope_ref, w1t_ref)
    second_ref[...] = back[:share]
    own_ref[...] = back[share:]


def row_kernel(
    mp_ref,
    own_ref,
    first_ref,
    second_ref,
    x_ref,
    member_ref,
    upstream_ref,
    gain_hbm,
    out_ref,
    gain_ref,
    semaphores,
    *,
    ring,
):
    copies = fetch((gain_hbm,), (gain_ref,), semaphores)
    rows = share_range(mp_ref, 0, ring, out_ref.shape[0])
    back = own_ref[...] + first_ref[: out_ref.shape[0], :].astype(f32) + second_ref[...].astype(f32)
    xhat, inverse_deviation = layer_statistics(x_ref[rows, :].astype(f32))
    copies[0].wait()
    dxhat = back * gain_ref[...][None, :]
    dx = inverse_deviation * (
        dxhat
        - jnp.mean(dxhat, axis=-1, keepdims=True)
        - xhat * jnp.mean(dxhat * xhat, axis=-1, keepdims=True)
    )
    upstream = jnp.dot(member_ref[rows, :], upstream_ref[...], precision=HIGHEST, preferred_element_type=f32)
    out_ref[...] = dx + upstream


def text_kernel(parts_ref, text_ref, grad_ref, loss_ref):
    text = text_ref[...].astype(f32)
    texts, width = text.shape
    parts = parts_ref[...].astype(f32)
    total = parts[:texts]
    for first in range(texts, parts.shape[0], texts):
        total = total + parts[first : first + texts]
    norm = jnp.sqrt(jnp.sum(text * text, axis=-1, keepdims=True) + eps)
    unit = text / norm
    dv = total[:, :width]
    grad_ref[...] = (dv - unit * jnp.sum(unit * dv, axis=-1, keepdims=True)) / norm
    loss_ref[...] = jnp.sum(total[:1, width:], axis=1, keepdims=True)


def call(kernel, outs, operands, scratch=(), flops=0, read=0):
    fetched = any(space is stored for space, _ in operands)
    extra = [pltpu.SemaphoreType.DMA((MOST_COPIES,))] if fetched else []
    return pl.pallas_call(
        kernel,
        out_shape=outs,
        in_specs=[space for space, _ in operands],
        out_specs=jax.tree.map(lambda _: whole, outs),
        scratch_shapes=list(scratch) + extra,
        compiler_params=pltpu.CompilerParams(vmem_limit_bytes=VMEM_LIMIT),
        cost_estimate=pl.CostEstimate(flops=flops, bytes_accessed=read, transcendentals=0),
    )(*[pltpu.with_memory_space_constraint(array, pltpu.HBM) if space is stored else array for space, array in operands])


def shape(dims, kind):
    return jax.ShapeDtypeStruct(dims, kind)


def exchange(block, axis):
    return lax.all_to_all(block, axis, split_axis=0, concat_axis=0, tiled=True)


def shards(
    patches,
    layer_norm_gain,
    layer_norm_bias,
    fc1_weight,
    fc1_bias,
    fc2_weight,
    counts,
    owners,
    text_embed,
    labels,
    logit_scale,
    logit_bias,
):
    dp_size = lax.axis_size("dp")
    mp_size = lax.axis_size("mp")
    dp_index = lax.axis_index("dp").astype(jnp.int32)[None]
    mp_index = lax.axis_index("mp").astype(jnp.int32)[None]
    loss_index = lax.axis_index("loss").astype(jnp.int32)[None]
    turn = jnp.where((mp_index + dp_index) % 2 == 0, 1, mp_size - 1)
    ring_place = jnp.concatenate([mp_index, turn])
    first_pairs, second_pairs = [], []
    for d in range(dp_size):
        for m in range(mp_size):
            step = 1 if (d + m) % 2 == 0 else mp_size - 1
            first_pairs.append((d * mp_size + m, d * mp_size + (m + step) % mp_size))
            second_pairs.append((d * mp_size + m, d * mp_size + (m - step) % mp_size))
    row_count, width = patches.shape
    hidden = fc1_weight.shape[1]
    share_rows = row_count // mp_size
    images = counts.shape[1]
    all_images = labels.shape[0]
    padded = -(-row_count // dp_size // 8) * 8
    fc1_t = fc1_weight.T
    matmul = 2 * row_count * width * hidden
    weight_bytes = 2 * width * hidden

    gain, bias, offset = layer_norm_gain, layer_norm_bias, fc1_bias
    gain_room, offset_room = pltpu.VMEM((width,), f32), pltpu.VMEM((hidden,), f32)
    plan_dims, counts_dims = owners.shape[1:], counts.shape
    first_room, second_room = pltpu.VMEM((hidden, width), bf16), pltpu.VMEM((hidden, width), bf16)

    outgoing = call(
        functools.partial(pack_kernel, padded=padded),
        shape((dp_size * padded, width), bf16),
        [(scalars, dp_index), (stored, owners), (stored, patches)],
        [pltpu.SMEM(plan_dims, jnp.int32), pltpu.VMEM((row_count, width), bf16)],
    )
    incoming = exchange(outgoing, "dp")

    patches, outgoing = lax.optimization_barrier((patches, outgoing))
    partial_sums = call(
        functools.partial(pool_kernel, share=1.0 / mp_size),
        shape((images, width), f32),
        [(scalars, dp_index)]
        + [(stored, array) for array in (counts, patches, gain, bias, offset, fc1_t, fc2_weight)],
        [
            pltpu.SMEM(counts_dims, jnp.int32),
            pltpu.VMEM((row_count, width), bf16),
            gain_room,
            gain_room,
            offset_room,
            first_room,
            second_room,
        ],
        flops=matmul,
        read=2 * weight_bytes,
    )
    slab_sums = jnp.sum(lax.all_gather(partial_sums, "mp", axis=0), axis=0)
    incoming, slab_sums = lax.optimization_barrier((incoming, slab_sums))
    slope, rows, member, text_copies = call(
        slope_kernel,
        (
            shape((row_count, hidden), f32),
            shape((row_count, width), bf16),
            shape((row_count, images), f32),
            shape((all_images, width), bf16),
        ),
        [(scalars, dp_index), (whole, incoming)]
        + [(stored, array) for array in (counts, owners, gain, bias, offset, text_embed, fc1_t)],
        [
            pltpu.SMEM(counts_dims, jnp.int32),
            pltpu.VMEM(plan_dims, jnp.int32),
            gain_room,
            gain_room,
            offset_room,
            pltpu.VMEM((images, width), bf16),
            first_room,
        ],
        flops=matmul,
        read=2 * weight_bytes,
    )
    texts = exchange(text_copies, "loss")
    slab_sums, slope = lax.optimization_barrier((slab_sums, slope))
    pieces = lax.all_gather(slab_sums, "dp", axis=0)
    upstream, parts, d_act, first_chunks = call(
        functools.partial(gradient_kernel, ring=mp_size),
        [
            shape((images, width), f32),
            shape((all_images, width + LANES), bf16),
            shape((2 * images, hidden), bf16),
            shape((2 * share_rows, width), bf16),
        ],
        [(scalars, array) for array in (loss_index, ring_place, logit_scale, logit_bias)]
        + [(whole, array) for array in (pieces, texts, member, slope)]
        + [(stored, array) for array in (counts, labels, fc2_weight, fc1_t)],
        [
            pltpu.SMEM(counts_dims, jnp.int32),
            pltpu.SMEM((all_images,), jnp.int32),
            second_room,
            first_room,
        ],
        flops=matmul,
        read=2 * weight_bytes,
    )
    first_received = lax.ppermute(first_chunks, ("dp", "mp"), first_pairs)
    second_chunk, own_back = call(
        functools.partial(rest_kernel, ring=mp_size),
        [shape((share_rows, width), f32)] * 2,
        [(scalars, ring_place), (whole, d_act), (whole, member), (whole, slope), (stored, fc1_t)],
        [first_room],
        flops=matmul // 2,
        read=weight_bytes,
    )
    second_sum = (second_chunk + first_received[share_rows:].astype(f32)).astype(bf16)
    second_received = lax.ppermute(second_sum, ("dp", "mp"), second_pairs)
    all_parts = exchange(parts, "loss")
    grad_text, loss = call(
        text_kernel,
        (shape((images, width), f32), shape((1, 1), f32)),
        [(whole, all_parts), (whole, text_embed)],
    )
    grad_rows = call(
        functools.partial(row_kernel, ring=mp_size),
        shape((share_rows, width), f32),
        [(scalars, ring_place)]
        + [(whole, array) for array in (own_back, first_received, second_received, rows, member, upstream)]
        + [(stored, gain)],
        [gain_room],
    )
    return (grad_rows, grad_text, loss[0, 0])


def solution(mesh):
    placed = (
        P(("dp", "loss"), None),
        P(),
        P(),
        P(None, "mp"),
        P("mp"),
        P("mp", None),
        P("loss", None),
        P("loss", None, None),
        P("loss", None),
        P(),
        P(),
        P(),
    )
    return jax.shard_map(
        shards,
        mesh=mesh,
        in_specs=placed,
        out_specs=(P(("dp", "loss", "mp"), None), P("loss", None), P()),
        check_vma=False,
    )
```

```python
import functools

import jax
import jax.numpy as jnp
from jax import lax
from jax.experimental import pallas as pl
from jax.experimental.pallas import tpu as pltpu
from jax.sharding import PartitionSpec as P

eps = 1e-06
grad_scale = 262144.0
gelu_coef = 0.7978845608028654
f32 = jnp.float32
bf16 = jnp.bfloat16
VMEM_LIMIT = 28 * 1024 * 1024
whole = pl.BlockSpec(memory_space=pltpu.VMEM)
scalars = pl.BlockSpec(memory_space=pltpu.SMEM)
stored = pl.BlockSpec(memory_space=pltpu.HBM)
NT = (((1,), (1,)), ((), ()))
TN = (((0,), (0,)), ((), ()))
LANES = 128
HIDDEN_STEP = 256
COPY_STEP = 384
PATCH_STEP = 80
PACK_STEP = 96
MOST_COPIES = 24
HIGHEST = lax.Precision.HIGHEST


def column_chunks(width, step):
    return [(first, min(step, width - first)) for first in range(0, width, step)]


def layer_statistics(floats):
    center = floats - jnp.mean(floats, axis=-1, keepdims=True)
    spread = jnp.mean(center * center, axis=-1, keepdims=True)
    inverse_deviation = lax.rsqrt(spread + eps)
    return center * inverse_deviation, inverse_deviation


def stacked_parts(values, many):
    parts = []
    for _ in range(many):
        part = values.astype(bf16).astype(f32)
        parts.append(part)
        values = values - part
    return jnp.concatenate(parts, axis=0).astype(bf16)


def fetch(sources, targets, semaphores, first=0):
    copies = [
        pltpu.make_async_copy(source, target, semaphores.at[first + k])
        for k, (source, target) in enumerate(zip(sources, targets))
    ]
    for copy in copies:
        copy.start()
    return copies


def row_pieces(array, step):
    return [array.at[pl.ds(first, many), :] for first, many in column_chunks(array.shape[0], step)]


def column_pieces(array, step):
    return [array.at[:, pl.ds(first, many)] for first, many in column_chunks(array.shape[1], step)]


def wait_all(copies):
    for copy in copies:
        copy.wait()


def quotient(values, by):
    return (values * (65536 // by + 1)) >> 16


def iota(dims, axis):
    return lax.broadcasted_iota(jnp.int32, dims, axis)


def one_hot(condition):
    return jnp.where(condition, 1.0, 0.0).astype(bf16)


def pack_kernel(dp_ref, owners_hbm, x_hbm, out_hbm, owners_ref, x_ref, out_ref, semaphores, *, padded):
    copies = fetch((owners_hbm.at[0],), (owners_ref,), semaphores)
    copies += fetch(row_pieces(x_hbm, PATCH_STEP), row_pieces(x_ref, PATCH_STEP), semaphores, 1)
    rows = x_ref.shape[0]
    slots = owners_ref.shape[0]
    block_rows = rows // slots
    block = quotient(iota((1, rows), 1), block_rows)
    within = iota((1, rows), 1) - block * block_rows
    owner = jnp.zeros((1, rows), jnp.int32)
    copies[0].wait()
    for b in range(slots):
        owner = jnp.where(block == b, owners_ref[dp_ref[0], b], owner)
    target = owner * padded + within
    wait_all(copies[1:])
    x = x_ref[...]
    written = []
    for first, many in column_chunks(out_ref.shape[0], PACK_STEP):
        pick = one_hot(first + iota((many, rows), 0) == target)
        out_ref[first : first + many, :] = jnp.dot(pick, x, preferred_element_type=f32).astype(bf16)
        piece = pl.ds(first, many)
        written += fetch((out_ref.at[piece, :],), (out_hbm.at[piece, :],), semaphores, len(copies) + len(written))
    wait_all(written)


def image_bounds(counts_ref, dims, axis):
    image = iota(dims, axis)
    starts = jnp.zeros(dims, jnp.int32)
    ends = jnp.zeros(dims, jnp.int32)
    first = jnp.int32(0)
    for j in range(counts_ref.shape[1]):
        last = first + counts_ref[0, j]
        starts = jnp.where(image == j, first, starts)
        ends = jnp.where(image == j, last, ends)
        first = last
    return starts, ends


def pool_kernel(
    dp_ref,
    counts_hbm,
    x_hbm,
    gain_hbm,
    bias_hbm,
    b1_hbm,
    w1t_hbm,
    w2_hbm,
    out_ref,
    counts_ref,
    x_ref,
    gain_ref,
    bias_ref,
    b1_ref,
    w1t_ref,
    w2_ref,
    semaphores,
    *,
    share,
):
    copies = fetch(
        (counts_hbm, gain_hbm, bias_hbm, b1_hbm, *row_pieces(x_hbm, PATCH_STEP)),
        (counts_ref, gain_ref, bias_ref, b1_ref, *row_pieces(x_ref, PATCH_STEP)),
        semaphores,
    )
    begin = len(copies)
    firsts = fetch(column_pieces(w1t_hbm, COPY_STEP), column_pieces(w1t_ref, COPY_STEP), semaphores, begin)
    begin += len(firsts)
    seconds = fetch(column_pieces(w2_hbm, COPY_STEP), column_pieces(w2_ref, COPY_STEP), semaphores, begin)
    wait_all(copies)
    rows = x_ref.shape[0]
    images = counts_ref.shape[1]
    position = dp_ref[0] * rows + iota((images, rows), 1)
    starts, ends = image_bounds(counts_ref, (images, 1), 0)
    member = one_hot((position >= starts) & (position < ends))
    x = x_ref[...]
    xhat, _ = layer_statistics(x.astype(f32))
    normed = (xhat * gain_ref[...][None, :] + bias_ref[...][None, :]).astype(bf16)
    offset = b1_ref[...][None, :]
    total = share * jnp.dot(member, x, preferred_element_type=f32)
    wait_all(firsts)
    for first, many in column_chunks(w1t_ref.shape[0], HIDDEN_STEP):
        cols = slice(first, first + many)
        pre = lax.dot_general(normed, w1t_ref[cols, :], NT, preferred_element_type=f32) + offset[:, cols]
        inner = gelu_coef * (pre + 0.044715 * pre * pre * pre)
        act = (0.5 * pre * (1.0 + jnp.tanh(inner))).astype(bf16)
        pooled = jnp.dot(member, act, preferred_element_type=f32)
        if first == 0:
            wait_all(seconds)
        both = stacked_parts(pooled, 2)
        product = jnp.dot(both, w2_ref[cols, :], preferred_element_type=f32)
        total = total + product[:images] + product[images:]
    out_ref[...] = total


def slope_kernel(
    dp_ref,
    in_ref,
    slabs_ref,
    text_ref,
    counts_hbm,
    owners_hbm,
    gain_hbm,
    bias_hbm,
    b1_hbm,
    w1t_hbm,
    slope_ref,
    rows_ref,
    member_ref,
    packed_ref,
    counts_ref,
    owners_ref,
    gain_ref,
    bias_ref,
    b1_ref,
    w1t_ref,
    semaphores,
):
    copies = fetch(
        (counts_hbm, owners_hbm.at[0], gain_hbm, bias_hbm, b1_hbm),
        (counts_ref, owners_ref, gain_ref, bias_ref, b1_ref),
        semaphores,
    )
    firsts = fetch(column_pieces(w1t_hbm, COPY_STEP), column_pieces(w1t_ref, COPY_STEP), semaphores, len(copies))
    rows = rows_ref.shape[0]
    slots = owners_ref.shape[0]
    block_rows = rows // slots
    padded = in_ref.shape[0] // slots
    source = quotient(iota((rows, 1), 0), block_rows)
    within = iota((rows, 1), 0) - source * block_rows
    pick = one_hot(iota((rows, in_ref.shape[0]), 1) == source * padded + within)
    x = jnp.dot(pick, in_ref[...], preferred_element_type=f32)
    rows_ref[...] = x.astype(bf16)
    wait_all(copies)
    images = member_ref.shape[1]
    total = slabs_ref[:images, :]
    for first in range(images, slabs_ref.shape[0], images):
        total = total + slabs_ref[first : first + images, :]
    packed = [stacked_parts(total, 2).astype(f32), text_ref[...].astype(f32)]
    packed_ref[...] = jnp.concatenate(packed, axis=0).astype(bf16)
    block = jnp.where(owners_ref[...] == dp_ref[0], iota((slots, slots), 1), 0)
    block = jnp.sum(block.astype(f32), axis=1, keepdims=True)
    by_source = one_hot(iota((rows, slots), 1) == source)
    block = jnp.dot(by_source, jnp.broadcast_to(block, (slots, LANES)).astype(bf16), preferred_element_type=f32)
    position = source * rows + block[:, :1].astype(jnp.int32) * block_rows + within
    starts, ends = image_bounds(counts_ref, (1, images), 1)
    member_ref[...] = jnp.where((position >= starts) & (position < ends), 1.0, 0.0)
    xhat, _ = layer_statistics(x)
    normed = (xhat * gain_ref[...][None, :] + bias_ref[...][None, :]).astype(bf16)
    offset = b1_ref[...][None, :]
    wait_all(firsts)
    for first, many in column_chunks(w1t_ref.shape[0], HIDDEN_STEP):
        cols = slice(first, first + many)
        pre = lax.dot_general(normed, w1t_ref[cols, :], NT, preferred_element_type=f32) + offset[:, cols]
        square = pre * pre
        tanh_part = jnp.tanh(gelu_coef * (pre + 0.044715 * square * pre))
        slope_ref[:, cols] = 0.5 * (1.0 + tanh_part) + 0.5 * pre * (
            1.0 - tanh_part * tanh_part
        ) * gelu_coef * (1.0 + 0.134145 * square)


def log_sigmoid(values):
    return jnp.minimum(values, 0.0) - jnp.log1p(jnp.exp(-jnp.abs(values)))


def gradient_kernel(
    loss_ref,
    mp_ref,
    scale_ref,
    shift_ref,
    packed_ref,
    member_ref,
    slope_ref,
    counts_hbm,
    labels_hbm,
    w2_hbm,
    w1t_hbm,
    upstream_ref,
    parts_hbm,
    d_act_ref,
    out_ref,
    w1t_ref,
    counts_ref,
    labels_ref,
    w2_ref,
    parts_ref,
    semaphores,
    *,
    ring,
):
    copies = fetch((counts_hbm, labels_hbm), (counts_ref, labels_ref), semaphores)
    begin = len(copies)
    seconds = fetch(column_pieces(w2_hbm, COPY_STEP), column_pieces(w2_ref, COPY_STEP), semaphores, begin)
    begin += len(seconds)
    firsts = fetch(column_pieces(w1t_hbm, COPY_STEP), column_pieces(w1t_ref, COPY_STEP), semaphores, begin)
    packed = packed_ref[...].astype(f32)
    images, width = upstream_ref.shape
    total = jnp.zeros((images, width), f32)
    blocks = []
    for first in range(0, packed.shape[0], 3 * images):
        total = total + (packed[first : first + images] + packed[first + images : first + 2 * images])
        blocks.append(packed[first + 2 * images : first + 3 * images])
    wide = jnp.concatenate(blocks, axis=0)
    texts = wide.astype(bf16)
    wait_all(copies)
    all_images = texts.shape[0]
    image = iota((images, 1), 0)
    count = jnp.zeros((images, 1), jnp.int32)
    label = jnp.zeros((images, 1), jnp.int32)
    for j in range(images):
        count = jnp.where(image == j, counts_ref[0, j], count)
        label = jnp.where(image == j, labels_ref[loss_ref[0] * images + j], label)
    count = count.astype(f32)
    embed = total / count
    norm_e = jnp.sqrt(jnp.sum(embed * embed, axis=-1, keepdims=True) + eps)
    unit_e = embed / norm_e
    norm_t = jnp.sqrt(jnp.sum(wide * wide, axis=-1, keepdims=True) + eps)
    inverse_t = (1.0 / norm_t).T
    scale = scale_ref[0]
    raw = lax.dot_general(stacked_parts(unit_e, 3), texts, NT, preferred_element_type=f32)
    raw = raw[:images] + raw[images : 2 * images] + raw[2 * images :]
    score = scale * (raw * inverse_t) + shift_ref[0]
    sign = jnp.where(iota((images, all_images), 1) == label, 1.0, -1.0)
    margin = sign * score
    dscore = -sign * jax.nn.sigmoid(-margin) / all_images
    du = jnp.dot(stacked_parts(dscore * inverse_t, 3), texts, preferred_element_type=f32)
    du = scale * (du[:images] + du[images : 2 * images] + du[2 * images :])
    dembed = (du - unit_e * jnp.sum(unit_e * du, axis=-1, keepdims=True)) / norm_e
    upstream_ref[...] = grad_scale * (dembed / count)
    scaled = stacked_parts(scale * dscore, 2).astype(f32)
    unit = stacked_parts(unit_e, 2).astype(f32)
    parts = lax.dot_general(
        jnp.concatenate([scaled[:images], scaled], axis=0).astype(bf16),
        jnp.concatenate([unit, unit[:images]], axis=0).astype(bf16),
        TN,
        preferred_element_type=f32,
    )
    parts_ref[:, :width] = parts.astype(bf16)
    loss = jnp.sum(jnp.sum(log_sigmoid(margin), axis=1, keepdims=True), axis=0, keepdims=True) / -all_images
    loss_high = loss.astype(bf16).astype(f32)
    lane = iota((all_images, LANES), 1)
    loss_lanes = jnp.where(lane == 0, loss_high, jnp.where(lane == 1, loss - loss_high, 0.0))
    parts_ref[:, width:] = loss_lanes.astype(bf16)
    written = fetch((parts_ref,), (parts_hbm,), semaphores, begin + len(firsts))
    wait_all(seconds)
    d_image = upstream_ref[...].astype(bf16)
    d_act = lax.dot_general(d_image, w2_ref[...], NT, preferred_element_type=f32)
    both = stacked_parts(d_act, 2)
    d_act_ref[...] = both
    wait_all(firsts)
    share = out_ref.shape[0] // 2
    back = back_of_shares(mp_ref, (mp_ref[1], 2), ring, share, member_ref, both, slope_ref, w1t_ref)
    out_ref[...] = back.astype(bf16)
    wait_all(written)


def share_range(mp_ref, step, ring, share):
    return pl.ds(pl.multiple_of(lax.rem(mp_ref[0] + step, ring) * share, share), share)


def back_of_shares(mp_ref, steps, ring, share, member_ref, d_act, slope_ref, w1t_ref):
    ranges = [share_range(mp_ref, step, ring, share) for step in steps]
    member = jnp.concatenate([member_ref[rows, :] for rows in ranges], axis=0)
    slope = jnp.concatenate([slope_ref[rows, :] for rows in ranges], axis=0)
    return back_rows(member, d_act, slope, w1t_ref[...])


def back_rows(member, both, slope, w1t):
    d_rows = jnp.dot(jnp.concatenate([member, member], axis=1).astype(bf16), both, preferred_element_type=f32)
    d_pre = (d_rows * slope).astype(bf16)
    return jnp.dot(d_pre, w1t, preferred_element_type=f32)


def second_kernel(mp_ref, d_act_ref, member_ref, slope_ref, w1t_ref, out_ref, *, ring):
    steps = (ring - mp_ref[1],)
    share = out_ref.shape[0]
    out_ref[...] = back_of_shares(mp_ref, steps, ring, share, member_ref, d_act_ref[...], slope_ref, w1t_ref)


def own_kernel(
    mp_ref,
    d_act_ref,
    member_ref,
    slope_ref,
    w1t_ref,
    first_ref,
    x_ref,
    upstream_ref,
    gain_hbm,
    back_ref,
    xhat_ref,
    deviation_ref,
    added_ref,
    gain_row_ref,
    gain_ref,
    semaphores,
    *,
    ring,
):
    copies = fetch((gain_hbm,), (gain_ref,), semaphores)
    share = back_ref.shape[0]
    rows = share_range(mp_ref, 0, ring, share)
    own = back_of_shares(mp_ref, (0,), ring, share, member_ref, d_act_ref[...], slope_ref, w1t_ref)
    back_ref[...] = own + first_ref[:share, :].astype(f32)
    xhat, inverse_deviation = layer_statistics(x_ref[rows, :].astype(f32))
    xhat_ref[...] = xhat
    deviation_ref[...] = inverse_deviation
    added_ref[...] = jnp.dot(member_ref[rows, :], upstream_ref[...], precision=HIGHEST, preferred_element_type=f32)
    wait_all(copies)
    gain_row_ref[...] = gain_ref[...][None, :]


def row_kernel(back_ref, second_ref, xhat_ref, deviation_ref, added_ref, gain_ref, out_ref):
    dxhat = (back_ref[...] + second_ref[...].astype(f32)) * gain_ref[...]
    xhat = xhat_ref[...]
    dx = deviation_ref[...] * (
        dxhat
        - jnp.mean(dxhat, axis=-1, keepdims=True)
        - xhat * jnp.mean(dxhat * xhat, axis=-1, keepdims=True)
    )
    out_ref[...] = dx + added_ref[...]


def text_kernel(parts_ref, text_ref, grad_ref, loss_ref):
    text = text_ref[...].astype(f32)
    texts, width = text.shape
    parts = parts_ref[...].astype(f32)
    total = parts[:texts]
    for first in range(texts, parts.shape[0], texts):
        total = total + parts[first : first + texts]
    norm = jnp.sqrt(jnp.sum(text * text, axis=-1, keepdims=True) + eps)
    unit = text / norm
    dv = total[:, :width]
    grad_ref[...] = (dv - unit * jnp.sum(unit * dv, axis=-1, keepdims=True)) / norm
    loss_ref[...] = jnp.sum(total[:1, width:], axis=1, keepdims=True)


def call(kernel, outs, operands, scratch=(), flops=0, read=0):
    copied = any(space is stored for space, _ in [*operands, *outs])
    extra = [pltpu.SemaphoreType.DMA((MOST_COPIES,))] if copied else []
    return pl.pallas_call(
        kernel,
        out_shape=[array for _, array in outs],
        in_specs=[space for space, _ in operands],
        out_specs=[space for space, _ in outs],
        scratch_shapes=list(scratch) + extra,
        compiler_params=pltpu.CompilerParams(vmem_limit_bytes=VMEM_LIMIT),
        cost_estimate=pl.CostEstimate(flops=flops, bytes_accessed=read, transcendentals=0),
    )(*[pltpu.with_memory_space_constraint(array, pltpu.HBM) if space is stored else array for space, array in operands])


def shape(dims, kind):
    return jax.ShapeDtypeStruct(dims, kind)


def exchange(block, axis):
    return lax.all_to_all(block, axis, split_axis=0, concat_axis=0, tiled=True)


def shards(
    patches,
    layer_norm_gain,
    layer_norm_bias,
    fc1_weight,
    fc1_bias,
    fc2_weight,
    counts,
    owners,
    text_embed,
    labels,
    logit_scale,
    logit_bias,
):
    dp_size = lax.axis_size("dp")
    mp_size = lax.axis_size("mp")
    dp_index = lax.axis_index("dp").astype(jnp.int32)[None]
    mp_index = lax.axis_index("mp").astype(jnp.int32)[None]
    loss_index = lax.axis_index("loss").astype(jnp.int32)[None]
    turn = jnp.where((mp_index + dp_index) % 2 == 0, 1, mp_size - 1)
    ring_place = jnp.concatenate([mp_index, turn])
    first_pairs, second_pairs = [], []
    for d in range(dp_size):
        for m in range(mp_size):
            step = 1 if (d + m) % 2 == 0 else mp_size - 1
            first_pairs.append((d * mp_size + m, d * mp_size + (m + step) % mp_size))
            second_pairs.append((d * mp_size + m, d * mp_size + (m - step) % mp_size))
    row_count, width = patches.shape
    hidden = fc1_weight.shape[1]
    share_rows = row_count // mp_size
    images = counts.shape[1]
    all_images = labels.shape[0]
    padded = -(-row_count // dp_size // 8) * 8
    fc1_t = fc1_weight.T
    matmul = 2 * row_count * width * hidden
    weight_bytes = 2 * width * hidden

    gain, bias, offset = layer_norm_gain, layer_norm_bias, fc1_bias
    gain_room, offset_room = pltpu.VMEM((width,), f32), pltpu.VMEM((hidden,), f32)
    plan_dims, counts_dims = owners.shape[1:], counts.shape
    first_room, second_room = pltpu.VMEM((hidden, width), bf16), pltpu.VMEM((hidden, width), bf16)

    swap = [(a * dp_size + b, b * dp_size + a) for a in range(dp_size) for b in range(dp_size)]
    text_block = lax.ppermute(text_embed, ("dp", "loss"), swap)

    (outgoing,) = call(
        functools.partial(pack_kernel, padded=padded),
        [(stored, shape((dp_size * padded, width), bf16))],
        [(scalars, dp_index), (stored, owners), (stored, patches)],
        [
            pltpu.SMEM(plan_dims, jnp.int32),
            pltpu.VMEM((row_count, width), bf16),
            pltpu.VMEM((dp_size * padded, width), bf16),
        ],
    )
    incoming = exchange(outgoing, "dp")

    patches, outgoing = lax.optimization_barrier((patches, outgoing))
    (partial_sums,) = call(
        functools.partial(pool_kernel, share=1.0 / mp_size),
        [(whole, shape((images, width), f32))],
        [(scalars, dp_index)]
        + [(stored, array) for array in (counts, patches, gain, bias, offset, fc1_t, fc2_weight)],
        [
            pltpu.SMEM(counts_dims, jnp.int32),
            pltpu.VMEM((row_count, width), bf16),
            gain_room,
            gain_room,
            offset_room,
            first_room,
            second_room,
        ],
        flops=matmul,
        read=2 * weight_bytes,
    )
    slab_pieces = lax.all_gather(partial_sums, "mp", axis=0, tiled=True)
    incoming, slab_pieces = lax.optimization_barrier((incoming, slab_pieces))
    slope, rows, member, packed = call(
        slope_kernel,
        [
            (whole, shape((row_count, hidden), f32)),
            (whole, shape((row_count, width), bf16)),
            (whole, shape((row_count, images), f32)),
            (whole, shape((3 * images, width), bf16)),
        ],
        [(scalars, dp_index), (whole, incoming), (whole, slab_pieces), (whole, text_block)]
        + [(stored, array) for array in (counts, owners, gain, bias, offset, fc1_t)],
        [
            pltpu.SMEM(counts_dims, jnp.int32),
            pltpu.VMEM(plan_dims, jnp.int32),
            gain_room,
            gain_room,
            offset_room,
            first_room,
        ],
        flops=matmul,
        read=2 * weight_bytes,
    )
    all_packed = lax.all_gather(packed, "dp", axis=0, tiled=True)
    upstream, parts, d_act, first_chunks, fc1_near = call(
        functools.partial(gradient_kernel, ring=mp_size),
        [
            (whole, shape((images, width), f32)),
            (stored, shape((all_images, width + LANES), bf16)),
            (whole, shape((2 * images, hidden), bf16)),
            (whole, shape((2 * share_rows, width), bf16)),
            (whole, shape((hidden, width), bf16)),
        ],
        [(scalars, array) for array in (loss_index, ring_place, logit_scale, logit_bias)]
        + [(whole, array) for array in (all_packed, member, slope)]
        + [(stored, array) for array in (counts, labels, fc2_weight, fc1_t)],
        [
            pltpu.SMEM(counts_dims, jnp.int32),
            pltpu.SMEM((all_images,), jnp.int32),
            second_room,
            pltpu.VMEM((all_images, width + LANES), bf16),
        ],
        flops=matmul,
        read=2 * weight_bytes,
    )
    first_received = lax.ppermute(first_chunks, ("dp", "mp"), first_pairs)
    factors = [(scalars, ring_place)] + [(whole, array) for array in (d_act, member, slope, fc1_near)]
    (second_chunk,) = call(
        functools.partial(second_kernel, ring=mp_size),
        [(whole, shape((share_rows, width), f32))],
        factors,
        flops=matmul // mp_size,
        read=weight_bytes,
    )
    second_sum = (second_chunk + first_received[share_rows:].astype(f32)).astype(bf16)
    second_received = lax.ppermute(second_sum, ("dp", "mp"), second_pairs)
    prepared = call(
        functools.partial(own_kernel, ring=mp_size),
        [(whole, shape((share_rows, width), f32))] * 2
        + [(whole, shape((share_rows, 1), f32)), (whole, shape((share_rows, width), f32)), (whole, shape((1, width), f32))],
        factors + [(whole, array) for array in (first_received, rows, upstream)] + [(stored, gain)],
        [gain_room],
        flops=matmul // mp_size,
        read=weight_bytes,
    )
    all_parts = exchange(parts, "loss")
    grad_text, loss = call(
        text_kernel,
        [(whole, shape((images, width), f32)), (whole, shape((1, 1), f32))],
        [(whole, all_parts), (whole, text_embed)],
    )
    own_back, *others = prepared
    own_back, grad_text, loss = lax.optimization_barrier((own_back, grad_text, loss))
    (grad_rows,) = call(
        row_kernel,
        [(whole, shape((share_rows, width), f32))],
        [(whole, array) for array in (own_back, second_received, *others)],
    )
    return (grad_rows, grad_text, loss[0, 0])


def solution(mesh):
    placed = (
        P(("dp", "loss"), None),
        P(),
        P(),
        P(None, "mp"),
        P("mp"),
        P("mp", None),
        P("loss", None),
        P("loss", None, None),
        P("loss", None),
        P(),
        P(),
        P(),
    )
    return jax.shard_map(
        shards,
        mesh=mesh,
        in_specs=placed,
        out_specs=(P(("dp", "loss", "mp"), None), P("loss", None), P()),
        check_vma=False,
    )
```

```python
import functools

import jax
import jax.numpy as jnp
from jax import lax
from jax.experimental import pallas as pl
from jax.experimental.pallas import tpu as pltpu
from jax.sharding import PartitionSpec as P

eps = 1e-06
grad_scale = 262144.0
gelu_coef = 0.7978845608028654
f32 = jnp.float32
bf16 = jnp.bfloat16
VMEM_LIMIT = 28 * 1024 * 1024
whole = pl.BlockSpec(memory_space=pltpu.VMEM)
scalars = pl.BlockSpec(memory_space=pltpu.SMEM)
stored = pl.BlockSpec(memory_space=pltpu.HBM)
NT = (((1,), (1,)), ((), ()))
TN = (((0,), (0,)), ((), ()))
LANES = 128
HIDDEN_STEP = 256
COPY_STEP = 384
PATCH_STEP = 80
PACK_STEP = 96
MOST_COPIES = 24
HIGHEST = lax.Precision.HIGHEST


def column_chunks(width, step):
    return [(first, min(step, width - first)) for first in range(0, width, step)]


def layer_statistics(floats):
    center = floats - jnp.mean(floats, axis=-1, keepdims=True)
    spread = jnp.mean(center * center, axis=-1, keepdims=True)
    inverse_deviation = lax.rsqrt(spread + eps)
    return center * inverse_deviation, inverse_deviation


def stacked_parts(values, many):
    parts = []
    for _ in range(many):
        part = values.astype(bf16).astype(f32)
        parts.append(part)
        values = values - part
    return jnp.concatenate(parts, axis=0).astype(bf16)


def fetch(sources, targets, semaphores, first=0):
    copies = [
        pltpu.make_async_copy(source, target, semaphores.at[first + k])
        for k, (source, target) in enumerate(zip(sources, targets))
    ]
    for copy in copies:
        copy.start()
    return copies


def row_pieces(array, step):
    return [array.at[pl.ds(first, many), :] for first, many in column_chunks(array.shape[0], step)]


def column_pieces(array, step):
    return [array.at[:, pl.ds(first, many)] for first, many in column_chunks(array.shape[1], step)]


def wait_all(copies):
    for copy in copies:
        copy.wait()


def quotient(values, by):
    return (values * (65536 // by + 1)) >> 16


def iota(dims, axis):
    return lax.broadcasted_iota(jnp.int32, dims, axis)


def one_hot(condition):
    return jnp.where(condition, 1.0, 0.0).astype(bf16)


def pack_kernel(dp_ref, owners_hbm, x_hbm, out_hbm, owners_ref, x_ref, out_ref, semaphores, *, padded):
    copies = fetch((owners_hbm.at[0],), (owners_ref,), semaphores)
    copies += fetch(row_pieces(x_hbm, PATCH_STEP), row_pieces(x_ref, PATCH_STEP), semaphores, 1)
    rows = x_ref.shape[0]
    slots = owners_ref.shape[0]
    block_rows = rows // slots
    block = quotient(iota((1, rows), 1), block_rows)
    within = iota((1, rows), 1) - block * block_rows
    owner = jnp.zeros((1, rows), jnp.int32)
    copies[0].wait()
    for b in range(slots):
        owner = jnp.where(block == b, owners_ref[dp_ref[0], b], owner)
    target = owner * padded + within
    wait_all(copies[1:])
    x = x_ref[...]
    written = []
    for first, many in column_chunks(out_ref.shape[0], PACK_STEP):
        pick = one_hot(first + iota((many, rows), 0) == target)
        out_ref[first : first + many, :] = jnp.dot(pick, x, preferred_element_type=f32).astype(bf16)
        piece = pl.ds(first, many)
        written += fetch((out_ref.at[piece, :],), (out_hbm.at[piece, :],), semaphores, len(copies) + len(written))
    wait_all(written)


def image_bounds(counts_ref, dims, axis):
    image = iota(dims, axis)
    starts = jnp.zeros(dims, jnp.int32)
    ends = jnp.zeros(dims, jnp.int32)
    first = jnp.int32(0)
    for j in range(counts_ref.shape[1]):
        last = first + counts_ref[0, j]
        starts = jnp.where(image == j, first, starts)
        ends = jnp.where(image == j, last, ends)
        first = last
    return starts, ends


def pool_kernel(
    dp_ref,
    counts_hbm,
    x_hbm,
    gain_hbm,
    bias_hbm,
    b1_hbm,
    w1t_hbm,
    w2_hbm,
    out_ref,
    counts_ref,
    x_ref,
    gain_ref,
    bias_ref,
    b1_ref,
    w1t_ref,
    w2_ref,
    semaphores,
    *,
    share,
):
    copies = fetch(
        (counts_hbm, gain_hbm, bias_hbm, b1_hbm, *row_pieces(x_hbm, PATCH_STEP)),
        (counts_ref, gain_ref, bias_ref, b1_ref, *row_pieces(x_ref, PATCH_STEP)),
        semaphores,
    )
    begin = len(copies)
    firsts = fetch(column_pieces(w1t_hbm, COPY_STEP), column_pieces(w1t_ref, COPY_STEP), semaphores, begin)
    begin += len(firsts)
    seconds = fetch(column_pieces(w2_hbm, COPY_STEP), column_pieces(w2_ref, COPY_STEP), semaphores, begin)
    wait_all(copies)
    rows = x_ref.shape[0]
    images = counts_ref.shape[1]
    position = dp_ref[0] * rows + iota((images, rows), 1)
    starts, ends = image_bounds(counts_ref, (images, 1), 0)
    member = one_hot((position >= starts) & (position < ends))
    x = x_ref[...]
    xhat, _ = layer_statistics(x.astype(f32))
    normed = (xhat * gain_ref[...][None, :] + bias_ref[...][None, :]).astype(bf16)
    offset = b1_ref[...][None, :]
    total = share * jnp.dot(member, x, preferred_element_type=f32)
    wait_all(firsts)
    for first, many in column_chunks(w1t_ref.shape[0], HIDDEN_STEP):
        cols = slice(first, first + many)
        pre = lax.dot_general(normed, w1t_ref[cols, :], NT, preferred_element_type=f32) + offset[:, cols]
        inner = gelu_coef * (pre + 0.044715 * pre * pre * pre)
        act = (0.5 * pre * (1.0 + jnp.tanh(inner))).astype(bf16)
        pooled = jnp.dot(member, act, preferred_element_type=f32)
        if first == 0:
            wait_all(seconds)
        both = stacked_parts(pooled, 2)
        product = jnp.dot(both, w2_ref[cols, :], preferred_element_type=f32)
        total = total + product[:images] + product[images:]
    out_ref[...] = total


def slope_kernel(
    dp_ref,
    mp_ref,
    in_ref,
    slabs_ref,
    text_ref,
    counts_hbm,
    owners_hbm,
    gain_hbm,
    bias_hbm,
    b1_hbm,
    w1t_hbm,
    slope_ref,
    own_ref,
    member_ref,
    packed_ref,
    counts_ref,
    owners_ref,
    gain_ref,
    bias_ref,
    b1_ref,
    w1t_ref,
    rows_ref,
    semaphores,
    *,
    ring,
):
    copies = fetch(
        (counts_hbm, owners_hbm.at[0], gain_hbm, bias_hbm, b1_hbm),
        (counts_ref, owners_ref, gain_ref, bias_ref, b1_ref),
        semaphores,
    )
    firsts = fetch(column_pieces(w1t_hbm, COPY_STEP), column_pieces(w1t_ref, COPY_STEP), semaphores, len(copies))
    rows = rows_ref.shape[0]
    slots = owners_ref.shape[0]
    block_rows = rows // slots
    padded = in_ref.shape[0] // slots
    source = quotient(iota((rows, 1), 0), block_rows)
    within = iota((rows, 1), 0) - source * block_rows
    pick = one_hot(iota((rows, in_ref.shape[0]), 1) == source * padded + within)
    x = jnp.dot(pick, in_ref[...], preferred_element_type=f32)
    rows_ref[...] = x
    own_ref[...] = rows_ref[share_range(mp_ref, 0, ring, own_ref.shape[0]), :].astype(bf16)
    wait_all(copies)
    images = member_ref.shape[1]
    total = slabs_ref[:images, :]
    for first in range(images, slabs_ref.shape[0], images):
        total = total + slabs_ref[first : first + images, :]
    packed = [stacked_parts(total, 2).astype(f32), text_ref[...].astype(f32)]
    packed_ref[...] = jnp.concatenate(packed, axis=0).astype(bf16)
    block = jnp.where(owners_ref[...] == dp_ref[0], iota((slots, slots), 1), 0)
    block = jnp.sum(block.astype(f32), axis=1, keepdims=True)
    by_source = one_hot(iota((rows, slots), 1) == source)
    block = jnp.dot(by_source, jnp.broadcast_to(block, (slots, LANES)).astype(bf16), preferred_element_type=f32)
    position = source * rows + block[:, :1].astype(jnp.int32) * block_rows + within
    starts, ends = image_bounds(counts_ref, (1, images), 1)
    member_ref[...] = jnp.where((position >= starts) & (position < ends), 1.0, 0.0)
    xhat, _ = layer_statistics(x)
    normed = (xhat * gain_ref[...][None, :] + bias_ref[...][None, :]).astype(bf16)
    offset = b1_ref[...][None, :]
    wait_all(firsts)
    for first, many in column_chunks(w1t_ref.shape[0], HIDDEN_STEP):
        cols = slice(first, first + many)
        pre = lax.dot_general(normed, w1t_ref[cols, :], NT, preferred_element_type=f32) + offset[:, cols]
        square = pre * pre
        tanh_part = jnp.tanh(gelu_coef * (pre + 0.044715 * square * pre))
        slope_ref[:, cols] = 0.5 * (1.0 + tanh_part) + 0.5 * pre * (
            1.0 - tanh_part * tanh_part
        ) * gelu_coef * (1.0 + 0.134145 * square)


def log_sigmoid(values):
    return jnp.minimum(values, 0.0) - jnp.log1p(jnp.exp(-jnp.abs(values)))


def gradient_kernel(
    loss_ref,
    mp_ref,
    scale_ref,
    shift_ref,
    packed_ref,
    member_ref,
    slope_ref,
    counts_hbm,
    labels_hbm,
    w2_hbm,
    w1t_hbm,
    upstream_ref,
    parts_hbm,
    d_act_ref,
    out_ref,
    counts_ref,
    labels_ref,
    w2_ref,
    w1t_ref,
    parts_ref,
    semaphores,
    *,
    ring,
):
    copies = fetch((counts_hbm, labels_hbm), (counts_ref, labels_ref), semaphores)
    begin = len(copies)
    seconds = fetch(column_pieces(w2_hbm, COPY_STEP), column_pieces(w2_ref, COPY_STEP), semaphores, begin)
    begin += len(seconds)
    firsts = fetch(column_pieces(w1t_hbm, COPY_STEP), column_pieces(w1t_ref, COPY_STEP), semaphores, begin)
    packed = packed_ref[...].astype(f32)
    images, width = upstream_ref.shape
    total = jnp.zeros((images, width), f32)
    blocks = []
    for first in range(0, packed.shape[0], 3 * images):
        total = total + (packed[first : first + images] + packed[first + images : first + 2 * images])
        blocks.append(packed[first + 2 * images : first + 3 * images])
    wide = jnp.concatenate(blocks, axis=0)
    texts = wide.astype(bf16)
    wait_all(copies)
    all_images = texts.shape[0]
    image = iota((images, 1), 0)
    count = jnp.zeros((images, 1), jnp.int32)
    label = jnp.zeros((images, 1), jnp.int32)
    for j in range(images):
        count = jnp.where(image == j, counts_ref[0, j], count)
        label = jnp.where(image == j, labels_ref[loss_ref[0] * images + j], label)
    count = count.astype(f32)
    embed = total / count
    norm_e = jnp.sqrt(jnp.sum(embed * embed, axis=-1, keepdims=True) + eps)
    unit_e = embed / norm_e
    norm_t = jnp.sqrt(jnp.sum(wide * wide, axis=-1, keepdims=True) + eps)
    inverse_t = (1.0 / norm_t).T
    scale = scale_ref[0]
    raw = lax.dot_general(stacked_parts(unit_e, 3), texts, NT, preferred_element_type=f32)
    raw = raw[:images] + raw[images : 2 * images] + raw[2 * images :]
    score = scale * (raw * inverse_t) + shift_ref[0]
    sign = jnp.where(iota((images, all_images), 1) == label, 1.0, -1.0)
    margin = sign * score
    dscore = -sign * jax.nn.sigmoid(-margin) / all_images
    du = jnp.dot(stacked_parts(dscore * inverse_t, 3), texts, preferred_element_type=f32)
    du = scale * (du[:images] + du[images : 2 * images] + du[2 * images :])
    dembed = (du - unit_e * jnp.sum(unit_e * du, axis=-1, keepdims=True)) / norm_e
    upstream_ref[...] = grad_scale * (dembed / count)
    scaled = stacked_parts(scale * dscore, 2).astype(f32)
    unit = stacked_parts(unit_e, 2).astype(f32)
    parts = lax.dot_general(
        jnp.concatenate([scaled[:images], scaled], axis=0).astype(bf16),
        jnp.concatenate([unit, unit[:images]], axis=0).astype(bf16),
        TN,
        preferred_element_type=f32,
    )
    parts_ref[:, :width] = parts.astype(bf16)
    loss = jnp.sum(jnp.sum(log_sigmoid(margin), axis=1, keepdims=True), axis=0, keepdims=True) / -all_images
    loss_high = loss.astype(bf16).astype(f32)
    lane = iota((all_images, LANES), 1)
    loss_lanes = jnp.where(lane == 0, loss_high, jnp.where(lane == 1, loss - loss_high, 0.0))
    parts_ref[:, width:] = loss_lanes.astype(bf16)
    written = fetch((parts_ref,), (parts_hbm,), semaphores, begin + len(firsts))
    wait_all(seconds)
    d_image = upstream_ref[...].astype(bf16)
    d_act = lax.dot_general(d_image, w2_ref[...], NT, preferred_element_type=f32)
    both = stacked_parts(d_act, 2)
    d_act_ref[...] = both
    wait_all(firsts)
    share = out_ref.shape[0] // 2
    back = back_of_shares(mp_ref, (mp_ref[1], 2), ring, share, member_ref, both, slope_ref, w1t_ref)
    out_ref[...] = back.astype(bf16)
    wait_all(written)


def share_range(mp_ref, step, ring, share):
    return pl.ds(pl.multiple_of(lax.rem(mp_ref[0] + step, ring) * share, share), share)


def back_of_shares(mp_ref, steps, ring, share, member_ref, d_act, slope_ref, w1t_ref):
    ranges = [share_range(mp_ref, step, ring, share) for step in steps]
    member = jnp.concatenate([member_ref[rows, :] for rows in ranges], axis=0)
    slope = jnp.concatenate([slope_ref[rows, :] for rows in ranges], axis=0)
    return back_rows(member, d_act, slope, w1t_ref[...])


def back_rows(member, both, slope, w1t):
    d_rows = jnp.dot(jnp.concatenate([member, member], axis=1).astype(bf16), both, preferred_element_type=f32)
    d_pre = (d_rows * slope).astype(bf16)
    return jnp.dot(d_pre, w1t, preferred_element_type=f32)


def second_kernel(mp_ref, d_act_ref, member_ref, slope_ref, w1t_hbm, out_ref, w1t_ref, semaphores, *, ring):
    wait_all(fetch(column_pieces(w1t_hbm, COPY_STEP), column_pieces(w1t_ref, COPY_STEP), semaphores))
    steps = (ring - mp_ref[1],)
    share = out_ref.shape[0]
    out_ref[...] = back_of_shares(mp_ref, steps, ring, share, member_ref, d_act_ref[...], slope_ref, w1t_ref)


def own_kernel(
    mp_ref,
    d_act_ref,
    member_ref,
    slope_ref,
    first_ref,
    parts_ref,
    w1t_hbm,
    gain_hbm,
    text_hbm,
    back_ref,
    gain_row_ref,
    grad_ref,
    loss_ref,
    w1t_ref,
    gain_ref,
    text_ref,
    semaphores,
    *,
    ring,
):
    copies = fetch((gain_hbm, text_hbm), (gain_ref, text_ref), semaphores)
    firsts = fetch(column_pieces(w1t_hbm, COPY_STEP), column_pieces(w1t_ref, COPY_STEP), semaphores, len(copies))
    wait_all(copies)
    gain_row_ref[...] = gain_ref[...][None, :]
    text = text_ref[...].astype(f32)
    texts, width = text.shape
    parts = parts_ref[...].astype(f32)
    total = parts[:texts]
    for first in range(texts, parts.shape[0], texts):
        total = total + parts[first : first + texts]
    norm = jnp.sqrt(jnp.sum(text * text, axis=-1, keepdims=True) + eps)
    unit = text / norm
    dv = total[:, :width]
    grad_ref[...] = (dv - unit * jnp.sum(unit * dv, axis=-1, keepdims=True)) / norm
    loss_ref[...] = jnp.sum(total[:1, width:], axis=1, keepdims=True)
    wait_all(firsts)
    share = back_ref.shape[0]
    own = back_of_shares(mp_ref, (0,), ring, share, member_ref, d_act_ref[...], slope_ref, w1t_ref)
    back_ref[...] = own + first_ref[:share, :].astype(f32)


def row_kernel(mp_ref, back_ref, second_ref, x_ref, member_ref, upstream_ref, gain_ref, out_ref, *, ring):
    rows = share_range(mp_ref, 0, ring, out_ref.shape[0])
    xhat, inverse_deviation = layer_statistics(x_ref[...].astype(f32))
    added = jnp.dot(member_ref[rows, :], upstream_ref[...], precision=HIGHEST, preferred_element_type=f32)
    dxhat = (back_ref[...] + second_ref[...].astype(f32)) * gain_ref[...]
    dx = inverse_deviation * (
        dxhat
        - jnp.mean(dxhat, axis=-1, keepdims=True)
        - xhat * jnp.mean(dxhat * xhat, axis=-1, keepdims=True)
    )
    out_ref[...] = dx + added


def call(kernel, outs, operands, scratch=(), flops=0, read=0):
    copied = any(space is stored for space, _ in [*operands, *outs])
    extra = [pltpu.SemaphoreType.DMA((MOST_COPIES,))] if copied else []
    return pl.pallas_call(
        kernel,
        out_shape=[array for _, array in outs],
        in_specs=[space for space, _ in operands],
        out_specs=[space for space, _ in outs],
        scratch_shapes=list(scratch) + extra,
        compiler_params=pltpu.CompilerParams(vmem_limit_bytes=VMEM_LIMIT),
        cost_estimate=pl.CostEstimate(flops=flops, bytes_accessed=read, transcendentals=0),
    )(*[pltpu.with_memory_space_constraint(array, pltpu.HBM) if space is stored else array for space, array in operands])


def shape(dims, kind):
    return jax.ShapeDtypeStruct(dims, kind)


def exchange(block, axis):
    return lax.all_to_all(block, axis, split_axis=0, concat_axis=0, tiled=True)


def shards(
    patches,
    layer_norm_gain,
    layer_norm_bias,
    fc1_weight,
    fc1_bias,
    fc2_weight,
    counts,
    owners,
    text_embed,
    labels,
    logit_scale,
    logit_bias,
):
    dp_size = lax.axis_size("dp")
    mp_size = lax.axis_size("mp")
    dp_index = lax.axis_index("dp").astype(jnp.int32)[None]
    mp_index = lax.axis_index("mp").astype(jnp.int32)[None]
    loss_index = lax.axis_index("loss").astype(jnp.int32)[None]
    turn = jnp.where((mp_index + dp_index) % 2 == 0, 1, mp_size - 1)
    ring_place = jnp.concatenate([mp_index, turn])
    first_pairs, second_pairs = [], []
    for d in range(dp_size):
        for m in range(mp_size):
            step = 1 if (d + m) % 2 == 0 else mp_size - 1
            first_pairs.append((d * mp_size + m, d * mp_size + (m + step) % mp_size))
            second_pairs.append((d * mp_size + m, d * mp_size + (m - step) % mp_size))
    row_count, width = patches.shape
    hidden = fc1_weight.shape[1]
    share_rows = row_count // mp_size
    images = counts.shape[1]
    all_images = labels.shape[0]
    padded = -(-row_count // dp_size // 8) * 8
    fc1_t = fc1_weight.T
    matmul = 2 * row_count * width * hidden
    weight_bytes = 2 * width * hidden

    gain, bias, offset = layer_norm_gain, layer_norm_bias, fc1_bias
    gain_room, offset_room = pltpu.VMEM((width,), f32), pltpu.VMEM((hidden,), f32)
    plan_dims, counts_dims = owners.shape[1:], counts.shape
    first_room, second_room = pltpu.VMEM((hidden, width), bf16), pltpu.VMEM((hidden, width), bf16)

    swap = [(a * dp_size + b, b * dp_size + a) for a in range(dp_size) for b in range(dp_size)]
    text_block = lax.ppermute(text_embed, ("dp", "loss"), swap)

    (outgoing,) = call(
        functools.partial(pack_kernel, padded=padded),
        [(stored, shape((dp_size * padded, width), bf16))],
        [(scalars, dp_index), (stored, owners), (stored, patches)],
        [
            pltpu.SMEM(plan_dims, jnp.int32),
            pltpu.VMEM((row_count, width), bf16),
            pltpu.VMEM((dp_size * padded, width), bf16),
        ],
    )
    incoming = exchange(outgoing, "dp")

    patches, outgoing, text_block = lax.optimization_barrier((patches, outgoing, text_block))
    (partial_sums,) = call(
        functools.partial(pool_kernel, share=1.0 / mp_size),
        [(whole, shape((images, width), f32))],
        [(scalars, dp_index)]
        + [(stored, array) for array in (counts, patches, gain, bias, offset, fc1_t, fc2_weight)],
        [
            pltpu.SMEM(counts_dims, jnp.int32),
            pltpu.VMEM((row_count, width), bf16),
            gain_room,
            gain_room,
            offset_room,
            first_room,
            second_room,
        ],
        flops=matmul,
        read=2 * weight_bytes,
    )
    slab_pieces = lax.all_gather(partial_sums, "mp", axis=0, tiled=True)
    incoming, slab_pieces = lax.optimization_barrier((incoming, slab_pieces))
    slope, own_rows, member, packed = call(
        functools.partial(slope_kernel, ring=mp_size),
        [
            (whole, shape((row_count, hidden), f32)),
            (whole, shape((share_rows, width), bf16)),
            (whole, shape((row_count, images), f32)),
            (whole, shape((3 * images, width), bf16)),
        ],
        [(scalars, dp_index), (scalars, ring_place), (whole, incoming), (whole, slab_pieces), (whole, text_block)]
        + [(stored, array) for array in (counts, owners, gain, bias, offset, fc1_t)],
        [
            pltpu.SMEM(counts_dims, jnp.int32),
            pltpu.VMEM(plan_dims, jnp.int32),
            gain_room,
            gain_room,
            offset_room,
            first_room,
            pltpu.VMEM((row_count, width), f32),
        ],
        flops=matmul,
        read=2 * weight_bytes,
    )
    all_packed = lax.all_gather(packed, "dp", axis=0, tiled=True)
    upstream, parts, d_act, first_chunks = call(
        functools.partial(gradient_kernel, ring=mp_size),
        [
            (whole, shape((images, width), f32)),
            (stored, shape((all_images, width + LANES), bf16)),
            (whole, shape((2 * images, hidden), bf16)),
            (whole, shape((2 * share_rows, width), bf16)),
        ],
        [(scalars, array) for array in (loss_index, ring_place, logit_scale, logit_bias)]
        + [(whole, array) for array in (all_packed, member, slope)]
        + [(stored, array) for array in (counts, labels, fc2_weight, fc1_t)],
        [
            pltpu.SMEM(counts_dims, jnp.int32),
            pltpu.SMEM((all_images,), jnp.int32),
            second_room,
            first_room,
            pltpu.VMEM((all_images, width + LANES), bf16),
        ],
        flops=matmul,
        read=2 * weight_bytes,
    )
    first_received = lax.ppermute(first_chunks, ("dp", "mp"), first_pairs)
    factors = [(scalars, ring_place)] + [(whole, array) for array in (d_act, member, slope)]
    (second_chunk,) = call(
        functools.partial(second_kernel, ring=mp_size),
        [(whole, shape((share_rows, width), f32))],
        factors + [(stored, fc1_t)],
        [first_room],
        flops=matmul // mp_size,
        read=weight_bytes,
    )
    second_sum = (second_chunk + first_received[share_rows:].astype(f32)).astype(bf16)
    second_received = lax.ppermute(second_sum, ("dp", "mp"), second_pairs)
    all_parts = exchange(parts, "loss")
    own_back, gain_row, grad_text, loss = call(
        functools.partial(own_kernel, ring=mp_size),
        [(whole, shape(dims, f32)) for dims in ((share_rows, width), (1, width), (images, width), (1, 1))],
        factors + [(whole, first_received), (whole, all_parts)] + [(stored, array) for array in (fc1_t, gain, text_embed)],
        [first_room, gain_room, pltpu.VMEM((images, width), bf16)],
        flops=matmul // mp_size,
        read=weight_bytes,
    )
    (grad_rows,) = call(
        functools.partial(row_kernel, ring=mp_size),
        [(whole, shape((share_rows, width), f32))],
        [(scalars, ring_place)]
        + [(whole, array) for array in (own_back, second_received, own_rows, member, upstream, gain_row)],
    )
    return (grad_rows, grad_text, loss[0, 0])


def solution(mesh):
    placed = (
        P(("dp", "loss"), None),
        P(),
        P(),
        P(None, "mp"),
        P("mp"),
        P("mp", None),
        P("loss", None),
        P("loss", None, None),
        P("loss", None),
        P(),
        P(),
        P(),
    )
    return jax.shard_map(
        shards,
        mesh=mesh,
        in_specs=placed,
        out_specs=(P(("dp", "loss", "mp"), None), P("loss", None), P()),
        check_vma=False,
    )
```

```python
import functools

import jax
import jax.numpy as jnp
from jax import lax
from jax.experimental import pallas as pl
from jax.experimental.pallas import tpu as pltpu
from jax.sharding import PartitionSpec as P

eps = 1e-06
grad_scale = 262144.0
gelu_coef = 0.7978845608028654
f32 = jnp.float32
bf16 = jnp.bfloat16
VMEM_LIMIT = 28 * 1024 * 1024
whole = pl.BlockSpec(memory_space=pltpu.VMEM)
scalars = pl.BlockSpec(memory_space=pltpu.SMEM)
stored = pl.BlockSpec(memory_space=pltpu.HBM)
NT = (((1,), (1,)), ((), ()))
TN = (((0,), (0,)), ((), ()))
LANES = 128
HIDDEN_STEP = 256
COPY_STEP = 384
PATCH_STEP = 80
PACK_STEP = 96
MOST_COPIES = 24
HIGHEST = lax.Precision.HIGHEST


def column_chunks(width, step):
    return [(first, min(step, width - first)) for first in range(0, width, step)]


def layer_statistics(floats):
    center = floats - jnp.mean(floats, axis=-1, keepdims=True)
    spread = jnp.mean(center * center, axis=-1, keepdims=True)
    inverse_deviation = lax.rsqrt(spread + eps)
    return center * inverse_deviation, inverse_deviation


def stacked_parts(values, many):
    parts = []
    for _ in range(many):
        part = values.astype(bf16).astype(f32)
        parts.append(part)
        values = values - part
    return jnp.concatenate(parts, axis=0).astype(bf16)


def fetch(sources, targets, semaphores, first=0):
    copies = [
        pltpu.make_async_copy(source, target, semaphores.at[first + k])
        for k, (source, target) in enumerate(zip(sources, targets))
    ]
    for copy in copies:
        copy.start()
    return copies


def row_pieces(array, step):
    return [array.at[pl.ds(first, many), :] for first, many in column_chunks(array.shape[0], step)]


def column_pieces(array, step):
    return [array.at[:, pl.ds(first, many)] for first, many in column_chunks(array.shape[1], step)]


def wait_all(copies):
    for copy in copies:
        copy.wait()


def quotient(values, by):
    return (values * (65536 // by + 1)) >> 16


def iota(dims, axis):
    return lax.broadcasted_iota(jnp.int32, dims, axis)


def one_hot(condition):
    return jnp.where(condition, 1.0, 0.0).astype(bf16)


def pack_kernel(dp_ref, owners_hbm, x_hbm, out_hbm, owners_ref, x_ref, out_ref, semaphores, *, padded):
    copies = fetch((owners_hbm.at[0],), (owners_ref,), semaphores)
    copies += fetch(row_pieces(x_hbm, PATCH_STEP), row_pieces(x_ref, PATCH_STEP), semaphores, 1)
    rows = x_ref.shape[0]
    slots = owners_ref.shape[0]
    block_rows = rows // slots
    block = quotient(iota((1, rows), 1), block_rows)
    within = iota((1, rows), 1) - block * block_rows
    owner = jnp.zeros((1, rows), jnp.int32)
    copies[0].wait()
    for b in range(slots):
        owner = jnp.where(block == b, owners_ref[dp_ref[0], b], owner)
    target = owner * padded + within
    wait_all(copies[1:])
    x = x_ref[...]
    written = []
    for first, many in column_chunks(out_ref.shape[0], PACK_STEP):
        pick = one_hot(first + iota((many, rows), 0) == target)
        out_ref[first : first + many, :] = jnp.dot(pick, x, preferred_element_type=f32).astype(bf16)
        piece = pl.ds(first, many)
        written += fetch((out_ref.at[piece, :],), (out_hbm.at[piece, :],), semaphores, len(copies) + len(written))
    wait_all(written)


def image_bounds(counts_ref, dims, axis):
    image = iota(dims, axis)
    starts = jnp.zeros(dims, jnp.int32)
    ends = jnp.zeros(dims, jnp.int32)
    first = jnp.int32(0)
    for j in range(counts_ref.shape[1]):
        last = first + counts_ref[0, j]
        starts = jnp.where(image == j, first, starts)
        ends = jnp.where(image == j, last, ends)
        first = last
    return starts, ends


def pool_kernel(
    dp_ref,
    counts_hbm,
    x_hbm,
    gain_hbm,
    bias_hbm,
    b1_hbm,
    w1t_hbm,
    w2_hbm,
    out_ref,
    counts_ref,
    x_ref,
    gain_ref,
    bias_ref,
    b1_ref,
    w1t_ref,
    w2_ref,
    semaphores,
    *,
    share,
):
    copies = fetch(
        (counts_hbm, gain_hbm, bias_hbm, b1_hbm, *row_pieces(x_hbm, PATCH_STEP)),
        (counts_ref, gain_ref, bias_ref, b1_ref, *row_pieces(x_ref, PATCH_STEP)),
        semaphores,
    )
    begin = len(copies)
    firsts = fetch(column_pieces(w1t_hbm, COPY_STEP), column_pieces(w1t_ref, COPY_STEP), semaphores, begin)
    begin += len(firsts)
    seconds = fetch(column_pieces(w2_hbm, COPY_STEP), column_pieces(w2_ref, COPY_STEP), semaphores, begin)
    wait_all(copies)
    rows = x_ref.shape[0]
    images = counts_ref.shape[1]
    position = dp_ref[0] * rows + iota((images, rows), 1)
    starts, ends = image_bounds(counts_ref, (images, 1), 0)
    member = one_hot((position >= starts) & (position < ends))
    x = x_ref[...]
    xhat, _ = layer_statistics(x.astype(f32))
    normed = (xhat * gain_ref[...][None, :] + bias_ref[...][None, :]).astype(bf16)
    offset = b1_ref[...][None, :]
    total = share * jnp.dot(member, x, preferred_element_type=f32)
    wait_all(firsts)
    for first, many in column_chunks(w1t_ref.shape[0], HIDDEN_STEP):
        cols = slice(first, first + many)
        pre = lax.dot_general(normed, w1t_ref[cols, :], NT, preferred_element_type=f32) + offset[:, cols]
        inner = gelu_coef * (pre + 0.044715 * pre * pre * pre)
        act = (0.5 * pre * (1.0 + jnp.tanh(inner))).astype(bf16)
        pooled = jnp.dot(member, act, preferred_element_type=f32)
        if first == 0:
            wait_all(seconds)
        both = stacked_parts(pooled, 2)
        product = jnp.dot(both, w2_ref[cols, :], preferred_element_type=f32)
        total = total + product[:images] + product[images:]
    out_ref[...] = total


def slope_kernel(
    dp_ref,
    mp_ref,
    in_ref,
    counts_hbm,
    owners_hbm,
    gain_hbm,
    bias_hbm,
    b1_hbm,
    text_hbm,
    w1t_hbm,
    slope_ref,
    own_ref,
    member_ref,
    texts_ref,
    counts_ref,
    owners_ref,
    gain_ref,
    bias_ref,
    b1_ref,
    text_ref,
    w1t_ref,
    rows_ref,
    semaphores,
    *,
    ring,
):
    copies = fetch(
        (counts_hbm, owners_hbm.at[0], gain_hbm, bias_hbm, b1_hbm, text_hbm),
        (counts_ref, owners_ref, gain_ref, bias_ref, b1_ref, text_ref),
        semaphores,
    )
    firsts = fetch(column_pieces(w1t_hbm, COPY_STEP), column_pieces(w1t_ref, COPY_STEP), semaphores, len(copies))
    rows = rows_ref.shape[0]
    slots = owners_ref.shape[0]
    block_rows = rows // slots
    padded = in_ref.shape[0] // slots
    source = quotient(iota((rows, 1), 0), block_rows)
    within = iota((rows, 1), 0) - source * block_rows
    pick = one_hot(iota((rows, in_ref.shape[0]), 1) == source * padded + within)
    x = jnp.dot(pick, in_ref[...], preferred_element_type=f32)
    rows_ref[...] = x
    own_ref[...] = rows_ref[share_range(mp_ref, 0, ring, own_ref.shape[0]), :].astype(bf16)
    wait_all(copies)
    images = member_ref.shape[1]
    text = text_ref[...].astype(f32)
    texts_ref[...] = jnp.concatenate([text] * (texts_ref.shape[0] // text.shape[0]), axis=0).astype(bf16)
    block = jnp.where(owners_ref[...] == dp_ref[0], iota((slots, slots), 1), 0)
    block = jnp.sum(block.astype(f32), axis=1, keepdims=True)
    by_source = one_hot(iota((rows, slots), 1) == source)
    block = jnp.dot(by_source, jnp.broadcast_to(block, (slots, LANES)).astype(bf16), preferred_element_type=f32)
    position = source * rows + block[:, :1].astype(jnp.int32) * block_rows + within
    starts, ends = image_bounds(counts_ref, (1, images), 1)
    member_ref[...] = jnp.where((position >= starts) & (position < ends), 1.0, 0.0)
    xhat, _ = layer_statistics(x)
    normed = (xhat * gain_ref[...][None, :] + bias_ref[...][None, :]).astype(bf16)
    offset = b1_ref[...][None, :]
    wait_all(firsts)
    for first, many in column_chunks(w1t_ref.shape[0], HIDDEN_STEP):
        cols = slice(first, first + many)
        pre = lax.dot_general(normed, w1t_ref[cols, :], NT, preferred_element_type=f32) + offset[:, cols]
        square = pre * pre
        tanh_part = jnp.tanh(gelu_coef * (pre + 0.044715 * square * pre))
        slope_ref[:, cols] = 0.5 * (1.0 + tanh_part) + 0.5 * pre * (
            1.0 - tanh_part * tanh_part
        ) * gelu_coef * (1.0 + 0.134145 * square)


def log_sigmoid(values):
    return jnp.minimum(values, 0.0) - jnp.log1p(jnp.exp(-jnp.abs(values)))


def gradient_kernel(
    loss_ref,
    mp_ref,
    scale_ref,
    shift_ref,
    pieces_ref,
    texts_ref,
    member_ref,
    slope_ref,
    counts_hbm,
    labels_hbm,
    w2_hbm,
    w1t_hbm,
    upstream_ref,
    parts_hbm,
    d_act_ref,
    out_ref,
    counts_ref,
    labels_ref,
    w2_ref,
    w1t_ref,
    parts_ref,
    semaphores,
    *,
    ring,
):
    copies = fetch((counts_hbm, labels_hbm), (counts_ref, labels_ref), semaphores)
    begin = len(copies)
    seconds = fetch(column_pieces(w2_hbm, COPY_STEP), column_pieces(w2_ref, COPY_STEP), semaphores, begin)
    begin += len(seconds)
    firsts = fetch(column_pieces(w1t_hbm, COPY_STEP), column_pieces(w1t_ref, COPY_STEP), semaphores, begin)
    images, width = upstream_ref.shape
    total = pieces_ref[:images, :]
    for first in range(images, pieces_ref.shape[0], images):
        total = total + pieces_ref[first : first + images, :]
    texts = texts_ref[...]
    wide = texts.astype(f32)
    wait_all(copies)
    all_images = texts.shape[0]
    image = iota((images, 1), 0)
    count = jnp.zeros((images, 1), jnp.int32)
    label = jnp.zeros((images, 1), jnp.int32)
    for j in range(images):
        count = jnp.where(image == j, counts_ref[0, j], count)
        label = jnp.where(image == j, labels_ref[loss_ref[0] * images + j], label)
    count = count.astype(f32)
    embed = total / count
    norm_e = jnp.sqrt(jnp.sum(embed * embed, axis=-1, keepdims=True) + eps)
    unit_e = embed / norm_e
    norm_t = jnp.sqrt(jnp.sum(wide * wide, axis=-1, keepdims=True) + eps)
    inverse_t = (1.0 / norm_t).T
    scale = scale_ref[0]
    raw = lax.dot_general(stacked_parts(unit_e, 3), texts, NT, preferred_element_type=f32)
    raw = raw[:images] + raw[images : 2 * images] + raw[2 * images :]
    score = scale * (raw * inverse_t) + shift_ref[0]
    sign = jnp.where(iota((images, all_images), 1) == label, 1.0, -1.0)
    margin = sign * score
    dscore = -sign * jax.nn.sigmoid(-margin) / all_images
    du = jnp.dot(stacked_parts(dscore * inverse_t, 3), texts, preferred_element_type=f32)
    du = scale * (du[:images] + du[images : 2 * images] + du[2 * images :])
    dembed = (du - unit_e * jnp.sum(unit_e * du, axis=-1, keepdims=True)) / norm_e
    upstream_ref[...] = grad_scale * (dembed / count)
    scaled = stacked_parts(scale * dscore, 2).astype(f32)
    unit = stacked_parts(unit_e, 2).astype(f32)
    parts = lax.dot_general(
        jnp.concatenate([scaled[:images], scaled], axis=0).astype(bf16),
        jnp.concatenate([unit, unit[:images]], axis=0).astype(bf16),
        TN,
        preferred_element_type=f32,
    )
    parts_ref[:, :width] = parts.astype(bf16)
    loss = jnp.sum(jnp.sum(log_sigmoid(margin), axis=1, keepdims=True), axis=0, keepdims=True) / -all_images
    loss_high = loss.astype(bf16).astype(f32)
    lane = iota((all_images, LANES), 1)
    loss_lanes = jnp.where(lane == 0, loss_high, jnp.where(lane == 1, loss - loss_high, 0.0))
    parts_ref[:, width:] = loss_lanes.astype(bf16)
    written = fetch((parts_ref,), (parts_hbm,), semaphores, begin + len(firsts))
    wait_all(seconds)
    d_image = upstream_ref[...].astype(bf16)
    d_act = lax.dot_general(d_image, w2_ref[...], NT, preferred_element_type=f32)
    both = stacked_parts(d_act, 2)
    d_act_ref[...] = both
    wait_all(firsts)
    share = out_ref.shape[0] // 2
    back = back_of_shares(mp_ref, (mp_ref[1], 2), ring, share, member_ref, both, slope_ref, w1t_ref)
    out_ref[...] = back.astype(bf16)
    wait_all(written)


def share_range(mp_ref, step, ring, share):
    return pl.ds(pl.multiple_of(lax.rem(mp_ref[0] + step, ring) * share, share), share)


def back_of_shares(mp_ref, steps, ring, share, member_ref, d_act, slope_ref, w1t_ref):
    ranges = [share_range(mp_ref, step, ring, share) for step in steps]
    member = jnp.concatenate([member_ref[rows, :] for rows in ranges], axis=0)
    slope = jnp.concatenate([slope_ref[rows, :] for rows in ranges], axis=0)
    return back_rows(member, d_act, slope, w1t_ref[...])


def back_rows(member, both, slope, w1t):
    d_rows = jnp.dot(jnp.concatenate([member, member], axis=1).astype(bf16), both, preferred_element_type=f32)
    d_pre = (d_rows * slope).astype(bf16)
    return jnp.dot(d_pre, w1t, preferred_element_type=f32)


def second_kernel(mp_ref, d_act_ref, member_ref, slope_ref, w1t_hbm, out_ref, w1t_ref, semaphores, *, ring):
    wait_all(fetch(column_pieces(w1t_hbm, COPY_STEP), column_pieces(w1t_ref, COPY_STEP), semaphores))
    steps = (ring - mp_ref[1],)
    share = out_ref.shape[0]
    out_ref[...] = back_of_shares(mp_ref, steps, ring, share, member_ref, d_act_ref[...], slope_ref, w1t_ref)


def own_kernel(
    mp_ref,
    d_act_ref,
    member_ref,
    slope_ref,
    first_ref,
    parts_ref,
    w1t_hbm,
    gain_hbm,
    text_hbm,
    back_ref,
    gain_row_ref,
    grad_ref,
    loss_ref,
    w1t_ref,
    gain_ref,
    text_ref,
    semaphores,
    *,
    ring,
):
    copies = fetch((gain_hbm, text_hbm), (gain_ref, text_ref), semaphores)
    firsts = fetch(column_pieces(w1t_hbm, COPY_STEP), column_pieces(w1t_ref, COPY_STEP), semaphores, len(copies))
    wait_all(copies)
    gain_row_ref[...] = gain_ref[...][None, :]
    text = text_ref[...].astype(f32)
    texts, width = text.shape
    parts = parts_ref[...].astype(f32)
    total = parts[:texts]
    for first in range(texts, parts.shape[0], texts):
        total = total + parts[first : first + texts]
    norm = jnp.sqrt(jnp.sum(text * text, axis=-1, keepdims=True) + eps)
    unit = text / norm
    dv = total[:, :width]
    grad_ref[...] = (dv - unit * jnp.sum(unit * dv, axis=-1, keepdims=True)) / norm
    loss_ref[...] = jnp.sum(total[:1, width:], axis=1, keepdims=True)
    wait_all(firsts)
    share = back_ref.shape[0]
    own = back_of_shares(mp_ref, (0,), ring, share, member_ref, d_act_ref[...], slope_ref, w1t_ref)
    back_ref[...] = own + first_ref[:share, :].astype(f32)


def row_kernel(mp_ref, back_ref, second_ref, x_ref, member_ref, upstream_ref, gain_ref, out_ref, *, ring):
    rows = share_range(mp_ref, 0, ring, out_ref.shape[0])
    xhat, inverse_deviation = layer_statistics(x_ref[...].astype(f32))
    added = jnp.dot(member_ref[rows, :], upstream_ref[...], precision=HIGHEST, preferred_element_type=f32)
    dxhat = (back_ref[...] + second_ref[...].astype(f32)) * gain_ref[...]
    dx = inverse_deviation * (
        dxhat
        - jnp.mean(dxhat, axis=-1, keepdims=True)
        - xhat * jnp.mean(dxhat * xhat, axis=-1, keepdims=True)
    )
    out_ref[...] = dx + added


def call(kernel, outs, operands, scratch=(), flops=0, read=0):
    copied = any(space is stored for space, _ in [*operands, *outs])
    extra = [pltpu.SemaphoreType.DMA((MOST_COPIES,))] if copied else []
    return pl.pallas_call(
        kernel,
        out_shape=[array for _, array in outs],
        in_specs=[space for space, _ in operands],
        out_specs=[space for space, _ in outs],
        scratch_shapes=list(scratch) + extra,
        compiler_params=pltpu.CompilerParams(vmem_limit_bytes=VMEM_LIMIT),
        cost_estimate=pl.CostEstimate(flops=flops, bytes_accessed=read, transcendentals=0),
    )(*[pltpu.with_memory_space_constraint(array, pltpu.HBM) if space is stored else array for space, array in operands])


def shape(dims, kind):
    return jax.ShapeDtypeStruct(dims, kind)


def exchange(block, axis):
    return lax.all_to_all(block, axis, split_axis=0, concat_axis=0, tiled=True)


def shards(
    patches,
    layer_norm_gain,
    layer_norm_bias,
    fc1_weight,
    fc1_bias,
    fc2_weight,
    counts,
    owners,
    text_embed,
    labels,
    logit_scale,
    logit_bias,
):
    dp_size = lax.axis_size("dp")
    mp_size = lax.axis_size("mp")
    dp_index = lax.axis_index("dp").astype(jnp.int32)[None]
    mp_index = lax.axis_index("mp").astype(jnp.int32)[None]
    loss_index = lax.axis_index("loss").astype(jnp.int32)[None]
    turn = jnp.where((mp_index + dp_index) % 2 == 0, 1, mp_size - 1)
    ring_place = jnp.concatenate([mp_index, turn])
    first_pairs, second_pairs = [], []
    for d in range(dp_size):
        for m in range(mp_size):
            step = 1 if (d + m) % 2 == 0 else mp_size - 1
            first_pairs.append((d * mp_size + m, d * mp_size + (m + step) % mp_size))
            second_pairs.append((d * mp_size + m, d * mp_size + (m - step) % mp_size))
    row_count, width = patches.shape
    hidden = fc1_weight.shape[1]
    share_rows = row_count // mp_size
    images = counts.shape[1]
    all_images = labels.shape[0]
    padded = -(-row_count // dp_size // 8) * 8
    fc1_t = fc1_weight.T
    matmul = 2 * row_count * width * hidden
    weight_bytes = 2 * width * hidden

    gain, bias, offset = layer_norm_gain, layer_norm_bias, fc1_bias
    gain_room, offset_room = pltpu.VMEM((width,), f32), pltpu.VMEM((hidden,), f32)
    plan_dims, counts_dims = owners.shape[1:], counts.shape
    first_room, second_room = pltpu.VMEM((hidden, width), bf16), pltpu.VMEM((hidden, width), bf16)

    (outgoing,) = call(
        functools.partial(pack_kernel, padded=padded),
        [(stored, shape((dp_size * padded, width), bf16))],
        [(scalars, dp_index), (stored, owners), (stored, patches)],
        [
            pltpu.SMEM(plan_dims, jnp.int32),
            pltpu.VMEM((row_count, width), bf16),
            pltpu.VMEM((dp_size * padded, width), bf16),
        ],
    )
    incoming = exchange(outgoing, "dp")

    patches, outgoing = lax.optimization_barrier((patches, outgoing))
    (partial_sums,) = call(
        functools.partial(pool_kernel, share=1.0 / mp_size),
        [(whole, shape((images, width), f32))],
        [(scalars, dp_index)]
        + [(stored, array) for array in (counts, patches, gain, bias, offset, fc1_t, fc2_weight)],
        [
            pltpu.SMEM(counts_dims, jnp.int32),
            pltpu.VMEM((row_count, width), bf16),
            gain_room,
            gain_room,
            offset_room,
            first_room,
            second_room,
        ],
        flops=matmul,
        read=2 * weight_bytes,
    )
    slab_sums = jnp.sum(lax.all_gather(partial_sums, "mp", axis=0), axis=0)
    incoming, slab_sums = lax.optimization_barrier((incoming, slab_sums))
    slope, own_rows, member, text_copies = call(
        functools.partial(slope_kernel, ring=mp_size),
        [
            (whole, shape((row_count, hidden), f32)),
            (whole, shape((share_rows, width), bf16)),
            (whole, shape((row_count, images), f32)),
            (whole, shape((all_images, width), bf16)),
        ],
        [(scalars, dp_index), (scalars, ring_place), (whole, incoming)]
        + [(stored, array) for array in (counts, owners, gain, bias, offset, text_embed, fc1_t)],
        [
            pltpu.SMEM(counts_dims, jnp.int32),
            pltpu.VMEM(plan_dims, jnp.int32),
            gain_room,
            gain_room,
            offset_room,
            pltpu.VMEM((images, width), bf16),
            first_room,
            pltpu.VMEM((row_count, width), f32),
        ],
        flops=matmul,
        read=2 * weight_bytes,
    )
    texts = exchange(text_copies, "loss")
    slab_sums, slope = lax.optimization_barrier((slab_sums, slope))
    pieces = lax.all_gather(slab_sums, "dp", axis=0, tiled=True)
    upstream, parts, d_act, first_chunks = call(
        functools.partial(gradient_kernel, ring=mp_size),
        [
            (whole, shape((images, width), f32)),
            (stored, shape((all_images, width + LANES), bf16)),
            (whole, shape((2 * images, hidden), bf16)),
            (whole, shape((2 * share_rows, width), bf16)),
        ],
        [(scalars, array) for array in (loss_index, ring_place, logit_scale, logit_bias)]
        + [(whole, array) for array in (pieces, texts, member, slope)]
        + [(stored, array) for array in (counts, labels, fc2_weight, fc1_t)],
        [
            pltpu.SMEM(counts_dims, jnp.int32),
            pltpu.SMEM((all_images,), jnp.int32),
            second_room,
            first_room,
            pltpu.VMEM((all_images, width + LANES), bf16),
        ],
        flops=matmul,
        read=2 * weight_bytes,
    )
    first_received = lax.ppermute(first_chunks, ("dp", "mp"), first_pairs)
    factors = [(scalars, ring_place)] + [(whole, array) for array in (d_act, member, slope)]
    (second_chunk,) = call(
        functools.partial(second_kernel, ring=mp_size),
        [(whole, shape((share_rows, width), f32))],
        factors + [(stored, fc1_t)],
        [first_room],
        flops=matmul // mp_size,
        read=weight_bytes,
    )
    second_sum = (second_chunk + first_received[share_rows:].astype(f32)).astype(bf16)
    second_received = lax.ppermute(second_sum, ("dp", "mp"), second_pairs)
    all_parts = exchange(parts, "loss")
    own_back, gain_row, grad_text, loss = call(
        functools.partial(own_kernel, ring=mp_size),
        [(whole, shape(dims, f32)) for dims in ((share_rows, width), (1, width), (images, width), (1, 1))],
        factors + [(whole, first_received), (whole, all_parts)] + [(stored, array) for array in (fc1_t, gain, text_embed)],
        [first_room, gain_room, pltpu.VMEM((images, width), bf16)],
        flops=matmul // mp_size,
        read=weight_bytes,
    )
    (grad_rows,) = call(
        functools.partial(row_kernel, ring=mp_size),
        [(whole, shape((share_rows, width), f32))],
        [(scalars, ring_place)]
        + [(whole, array) for array in (own_back, second_received, own_rows, member, upstream, gain_row)],
    )
    return (grad_rows, grad_text, loss[0, 0])


def solution(mesh):
    placed = (
        P(("dp", "loss"), None),
        P(),
        P(),
        P(None, "mp"),
        P("mp"),
        P("mp", None),
        P("loss", None),
        P("loss", None, None),
        P("loss", None),
        P(),
        P(),
        P(),
    )
    return jax.shard_map(
        shards,
        mesh=mesh,
        in_specs=placed,
        out_specs=(P(("dp", "loss", "mp"), None), P("loss", None), P()),
        check_vma=False,
    )
```

```python
import functools

import jax
import jax.numpy as jnp
from jax import lax
from jax.experimental import pallas as pl
from jax.experimental.pallas import tpu as pltpu
from jax.sharding import PartitionSpec as P

eps = 1e-06
grad_scale = 262144.0
gelu_coef = 0.7978845608028654
f32 = jnp.float32
bf16 = jnp.bfloat16
VMEM_LIMIT = 28 * 1024 * 1024
whole = pl.BlockSpec(memory_space=pltpu.VMEM)
scalars = pl.BlockSpec(memory_space=pltpu.SMEM)
stored = pl.BlockSpec(memory_space=pltpu.HBM)
NT = (((1,), (1,)), ((), ()))
TN = (((0,), (0,)), ((), ()))
LANES = 128
HIDDEN_STEP = 256
COPY_STEP = 384
PATCH_STEP = 80
PACK_STEP = 96
MOST_COPIES = 24
HIGHEST = lax.Precision.HIGHEST


def column_chunks(width, step):
    return [(first, min(step, width - first)) for first in range(0, width, step)]


def layer_statistics(floats):
    center = floats - jnp.mean(floats, axis=-1, keepdims=True)
    spread = jnp.mean(center * center, axis=-1, keepdims=True)
    inverse_deviation = lax.rsqrt(spread + eps)
    return center * inverse_deviation, inverse_deviation


def stacked_parts(values, many):
    parts = []
    for _ in range(many):
        part = values.astype(bf16).astype(f32)
        parts.append(part)
        values = values - part
    return jnp.concatenate(parts, axis=0).astype(bf16)


def fetch(sources, targets, semaphores, first=0):
    copies = [
        pltpu.make_async_copy(source, target, semaphores.at[first + k])
        for k, (source, target) in enumerate(zip(sources, targets))
    ]
    for copy in copies:
        copy.start()
    return copies


def row_pieces(array, step):
    return [array.at[pl.ds(first, many), :] for first, many in column_chunks(array.shape[0], step)]


def column_pieces(array, step):
    return [array.at[:, pl.ds(first, many)] for first, many in column_chunks(array.shape[1], step)]


def wait_all(copies):
    for copy in copies:
        copy.wait()


def quotient(values, by):
    return (values * (65536 // by + 1)) >> 16


def iota(dims, axis):
    return lax.broadcasted_iota(jnp.int32, dims, axis)


def one_hot(condition):
    return jnp.where(condition, 1.0, 0.0).astype(bf16)


def pack_kernel(dp_ref, owners_hbm, x_hbm, out_hbm, owners_ref, x_ref, out_ref, semaphores, *, padded):
    copies = fetch((owners_hbm.at[0],), (owners_ref,), semaphores)
    copies += fetch(row_pieces(x_hbm, PATCH_STEP), row_pieces(x_ref, PATCH_STEP), semaphores, 1)
    rows = x_ref.shape[0]
    slots = owners_ref.shape[0]
    block_rows = rows // slots
    block = quotient(iota((1, rows), 1), block_rows)
    within = iota((1, rows), 1) - block * block_rows
    owner = jnp.zeros((1, rows), jnp.int32)
    copies[0].wait()
    for b in range(slots):
        owner = jnp.where(block == b, owners_ref[dp_ref[0], b], owner)
    target = owner * padded + within
    wait_all(copies[1:])
    x = x_ref[...]
    written = []
    for first, many in column_chunks(out_ref.shape[0], PACK_STEP):
        pick = one_hot(first + iota((many, rows), 0) == target)
        out_ref[first : first + many, :] = jnp.dot(pick, x, preferred_element_type=f32).astype(bf16)
        piece = pl.ds(first, many)
        written += fetch((out_ref.at[piece, :],), (out_hbm.at[piece, :],), semaphores, len(copies) + len(written))
    wait_all(written)


def image_bounds(counts_ref, dims, axis):
    image = iota(dims, axis)
    starts = jnp.zeros(dims, jnp.int32)
    ends = jnp.zeros(dims, jnp.int32)
    first = jnp.int32(0)
    for j in range(counts_ref.shape[1]):
        last = first + counts_ref[0, j]
        starts = jnp.where(image == j, first, starts)
        ends = jnp.where(image == j, last, ends)
        first = last
    return starts, ends


def pool_kernel(
    dp_ref,
    counts_hbm,
    x_hbm,
    gain_hbm,
    bias_hbm,
    b1_hbm,
    w1t_hbm,
    w2_hbm,
    out_ref,
    counts_ref,
    x_ref,
    gain_ref,
    bias_ref,
    b1_ref,
    w1t_ref,
    w2_ref,
    semaphores,
    *,
    share,
):
    copies = fetch(
        (counts_hbm, gain_hbm, bias_hbm, b1_hbm, *row_pieces(x_hbm, PATCH_STEP)),
        (counts_ref, gain_ref, bias_ref, b1_ref, *row_pieces(x_ref, PATCH_STEP)),
        semaphores,
    )
    begin = len(copies)
    firsts = fetch(column_pieces(w1t_hbm, COPY_STEP), column_pieces(w1t_ref, COPY_STEP), semaphores, begin)
    begin += len(firsts)
    seconds = fetch(column_pieces(w2_hbm, COPY_STEP), column_pieces(w2_ref, COPY_STEP), semaphores, begin)
    wait_all(copies)
    rows = x_ref.shape[0]
    images = counts_ref.shape[1]
    position = dp_ref[0] * rows + iota((images, rows), 1)
    starts, ends = image_bounds(counts_ref, (images, 1), 0)
    member = one_hot((position >= starts) & (position < ends))
    x = x_ref[...]
    xhat, _ = layer_statistics(x.astype(f32))
    normed = (xhat * gain_ref[...][None, :] + bias_ref[...][None, :]).astype(bf16)
    offset = b1_ref[...][None, :]
    total = share * jnp.dot(member, x, preferred_element_type=f32)
    wait_all(firsts)
    for first, many in column_chunks(w1t_ref.shape[0], HIDDEN_STEP):
        cols = slice(first, first + many)
        pre = lax.dot_general(normed, w1t_ref[cols, :], NT, preferred_element_type=f32) + offset[:, cols]
        inner = gelu_coef * (pre + 0.044715 * pre * pre * pre)
        act = (0.5 * pre * (1.0 + jnp.tanh(inner))).astype(bf16)
        pooled = jnp.dot(member, act, preferred_element_type=f32)
        if first == 0:
            wait_all(seconds)
        both = stacked_parts(pooled, 2)
        product = jnp.dot(both, w2_ref[cols, :], preferred_element_type=f32)
        total = total + product[:images] + product[images:]
    out_ref[...] = total


def slope_kernel(
    dp_ref,
    mp_ref,
    in_ref,
    counts_hbm,
    owners_hbm,
    gain_hbm,
    bias_hbm,
    b1_hbm,
    text_hbm,
    w1t_hbm,
    slope_ref,
    own_ref,
    member_ref,
    texts_ref,
    counts_ref,
    owners_ref,
    gain_ref,
    bias_ref,
    b1_ref,
    text_ref,
    w1t_ref,
    semaphores,
):
    copies = fetch(
        (counts_hbm, owners_hbm.at[0], gain_hbm, bias_hbm, b1_hbm, text_hbm),
        (counts_ref, owners_ref, gain_ref, bias_ref, b1_ref, text_ref),
        semaphores,
    )
    firsts = fetch(column_pieces(w1t_hbm, COPY_STEP), column_pieces(w1t_ref, COPY_STEP), semaphores, len(copies))
    rows = slope_ref.shape[0]
    slots = owners_ref.shape[0]
    block_rows = rows // slots
    padded = in_ref.shape[0] // slots
    source = quotient(iota((rows, 1), 0), block_rows)
    within = iota((rows, 1), 0) - source * block_rows
    pick = one_hot(iota((rows, in_ref.shape[0]), 1) == source * padded + within)
    x = jnp.dot(pick, in_ref[...], preferred_element_type=f32)
    share = own_ref.shape[0]
    own = mp_ref[0] * share + iota((share, 1), 0)
    own_source = quotient(own, block_rows)
    own_pick = one_hot(iota((share, in_ref.shape[0]), 1) == own_source * padded + own - own_source * block_rows)
    own_ref[...] = jnp.dot(own_pick, in_ref[...], preferred_element_type=f32).astype(bf16)
    wait_all(copies)
    images = member_ref.shape[1]
    text = text_ref[...].astype(f32)
    texts_ref[...] = jnp.concatenate([text] * (texts_ref.shape[0] // text.shape[0]), axis=0).astype(bf16)
    block = jnp.where(owners_ref[...] == dp_ref[0], iota((slots, slots), 1), 0)
    block = jnp.sum(block.astype(f32), axis=1, keepdims=True)
    by_source = one_hot(iota((rows, slots), 1) == source)
    block = jnp.dot(by_source, jnp.broadcast_to(block, (slots, LANES)).astype(bf16), preferred_element_type=f32)
    position = source * rows + block[:, :1].astype(jnp.int32) * block_rows + within
    starts, ends = image_bounds(counts_ref, (1, images), 1)
    member_ref[...] = jnp.where((position >= starts) & (position < ends), 1.0, 0.0)
    xhat, _ = layer_statistics(x)
    normed = (xhat * gain_ref[...][None, :] + bias_ref[...][None, :]).astype(bf16)
    offset = b1_ref[...][None, :]
    wait_all(firsts)
    for first, many in column_chunks(w1t_ref.shape[0], HIDDEN_STEP):
        cols = slice(first, first + many)
        pre = lax.dot_general(normed, w1t_ref[cols, :], NT, preferred_element_type=f32) + offset[:, cols]
        square = pre * pre
        tanh_part = jnp.tanh(gelu_coef * (pre + 0.044715 * square * pre))
        slope_ref[:, cols] = 0.5 * (1.0 + tanh_part) + 0.5 * pre * (
            1.0 - tanh_part * tanh_part
        ) * gelu_coef * (1.0 + 0.134145 * square)


def log_sigmoid(values):
    return jnp.minimum(values, 0.0) - jnp.log1p(jnp.exp(-jnp.abs(values)))


def gradient_kernel(
    loss_ref,
    mp_ref,
    scale_ref,
    shift_ref,
    pieces_ref,
    texts_ref,
    member_ref,
    slope_ref,
    counts_hbm,
    labels_hbm,
    w2_hbm,
    w1t_hbm,
    upstream_ref,
    parts_hbm,
    d_act_ref,
    out_ref,
    counts_ref,
    labels_ref,
    w2_ref,
    w1t_ref,
    parts_ref,
    semaphores,
    *,
    ring,
):
    copies = fetch((counts_hbm, labels_hbm), (counts_ref, labels_ref), semaphores)
    begin = len(copies)
    seconds = fetch(column_pieces(w2_hbm, COPY_STEP), column_pieces(w2_ref, COPY_STEP), semaphores, begin)
    begin += len(seconds)
    firsts = fetch(column_pieces(w1t_hbm, COPY_STEP), column_pieces(w1t_ref, COPY_STEP), semaphores, begin)
    images, width = upstream_ref.shape
    total = pieces_ref[:images, :]
    for first in range(images, pieces_ref.shape[0], images):
        total = total + pieces_ref[first : first + images, :]
    texts = texts_ref[...]
    wide = texts.astype(f32)
    wait_all(copies)
    all_images = texts.shape[0]
    image = iota((images, 1), 0)
    count = jnp.zeros((images, 1), jnp.int32)
    label = jnp.zeros((images, 1), jnp.int32)
    for j in range(images):
        count = jnp.where(image == j, counts_ref[0, j], count)
        label = jnp.where(image == j, labels_ref[loss_ref[0] * images + j], label)
    count = count.astype(f32)
    embed = total / count
    norm_e = jnp.sqrt(jnp.sum(embed * embed, axis=-1, keepdims=True) + eps)
    unit_e = embed / norm_e
    norm_t = jnp.sqrt(jnp.sum(wide * wide, axis=-1, keepdims=True) + eps)
    inverse_t = (1.0 / norm_t).T
    scale = scale_ref[0]
    raw = lax.dot_general(stacked_parts(unit_e, 3), texts, NT, preferred_element_type=f32)
    raw = raw[:images] + raw[images : 2 * images] + raw[2 * images :]
    score = scale * (raw * inverse_t) + shift_ref[0]
    sign = jnp.where(iota((images, all_images), 1) == label, 1.0, -1.0)
    margin = sign * score
    dscore = -sign * jax.nn.sigmoid(-margin) / all_images
    du = jnp.dot(stacked_parts(dscore * inverse_t, 3), texts, preferred_element_type=f32)
    du = scale * (du[:images] + du[images : 2 * images] + du[2 * images :])
    dembed = (du - unit_e * jnp.sum(unit_e * du, axis=-1, keepdims=True)) / norm_e
    upstream_ref[...] = grad_scale * (dembed / count)
    scaled = stacked_parts(scale * dscore, 2).astype(f32)
    unit = stacked_parts(unit_e, 2).astype(f32)
    parts = lax.dot_general(
        jnp.concatenate([scaled[:images], scaled], axis=0).astype(bf16),
        jnp.concatenate([unit, unit[:images]], axis=0).astype(bf16),
        TN,
        preferred_element_type=f32,
    )
    parts_ref[:, :width] = parts.astype(bf16)
    loss = jnp.sum(jnp.sum(log_sigmoid(margin), axis=1, keepdims=True), axis=0, keepdims=True) / -all_images
    loss_high = loss.astype(bf16).astype(f32)
    lane = iota((all_images, LANES), 1)
    loss_lanes = jnp.where(lane == 0, loss_high, jnp.where(lane == 1, loss - loss_high, 0.0))
    parts_ref[:, width:] = loss_lanes.astype(bf16)
    written = fetch((parts_ref,), (parts_hbm,), semaphores, begin + len(firsts))
    wait_all(seconds)
    d_image = upstream_ref[...].astype(bf16)
    d_act = lax.dot_general(d_image, w2_ref[...], NT, preferred_element_type=f32)
    both = stacked_parts(d_act, 2)
    d_act_ref[...] = both
    wait_all(firsts)
    share = out_ref.shape[0] // 2
    back = back_of_shares(mp_ref, (mp_ref[1], 2), ring, share, member_ref, both, slope_ref, w1t_ref)
    out_ref[...] = back.astype(bf16)
    wait_all(written)


def share_range(mp_ref, step, ring, share):
    return pl.ds(pl.multiple_of(lax.rem(mp_ref[0] + step, ring) * share, share), share)


def back_of_shares(mp_ref, steps, ring, share, member_ref, d_act, slope_ref, w1t_ref):
    ranges = [share_range(mp_ref, step, ring, share) for step in steps]
    member = jnp.concatenate([member_ref[rows, :] for rows in ranges], axis=0)
    slope = jnp.concatenate([slope_ref[rows, :] for rows in ranges], axis=0)
    return back_rows(member, d_act, slope, w1t_ref[...])


def back_rows(member, both, slope, w1t):
    d_rows = jnp.dot(jnp.concatenate([member, member], axis=1).astype(bf16), both, preferred_element_type=f32)
    d_pre = (d_rows * slope).astype(bf16)
    return jnp.dot(d_pre, w1t, preferred_element_type=f32)


def rest_kernel(mp_ref, d_act_ref, member_ref, slope_ref, w1t_hbm, second_ref, own_ref, w1t_ref, semaphores, *, ring):
    wait_all(fetch(column_pieces(w1t_hbm, COPY_STEP), column_pieces(w1t_ref, COPY_STEP), semaphores))
    steps = (ring - mp_ref[1], 0)
    share = own_ref.shape[0]
    back = back_of_shares(mp_ref, steps, ring, share, member_ref, d_act_ref[...], slope_ref, w1t_ref)
    second_ref[...] = back[:share]
    own_ref[...] = back[share:]


def text_kernel(parts_ref, text_ref, grad_ref, loss_ref):
    text = text_ref[...].astype(f32)
    texts, width = text.shape
    parts = parts_ref[...].astype(f32)
    total = parts[:texts]
    for first in range(texts, parts.shape[0], texts):
        total = total + parts[first : first + texts]
    norm = jnp.sqrt(jnp.sum(text * text, axis=-1, keepdims=True) + eps)
    unit = text / norm
    dv = total[:, :width]
    grad_ref[...] = (dv - unit * jnp.sum(unit * dv, axis=-1, keepdims=True)) / norm
    loss_ref[...] = jnp.sum(total[:1, width:], axis=1, keepdims=True)


def row_kernel(
    mp_ref,
    own_ref,
    first_ref,
    second_ref,
    x_ref,
    member_ref,
    upstream_ref,
    gain_hbm,
    out_ref,
    gain_ref,
    semaphores,
    *,
    ring,
):
    copies = fetch((gain_hbm,), (gain_ref,), semaphores)
    share = out_ref.shape[0]
    rows = share_range(mp_ref, 0, ring, share)
    xhat, inverse_deviation = layer_statistics(x_ref[...].astype(f32))
    added = jnp.dot(member_ref[rows, :], upstream_ref[...], precision=HIGHEST, preferred_element_type=f32)
    back = own_ref[...] + first_ref[:share, :].astype(f32) + second_ref[...].astype(f32)
    wait_all(copies)
    dxhat = back * gain_ref[...][None, :]
    dx = inverse_deviation * (
        dxhat
        - jnp.mean(dxhat, axis=-1, keepdims=True)
        - xhat * jnp.mean(dxhat * xhat, axis=-1, keepdims=True)
    )
    out_ref[...] = dx + added


def call(kernel, outs, operands, scratch=(), flops=0, read=0):
    copied = any(space is stored for space, _ in [*operands, *outs])
    extra = [pltpu.SemaphoreType.DMA((MOST_COPIES,))] if copied else []
    return pl.pallas_call(
        kernel,
        out_shape=[array for _, array in outs],
        in_specs=[space for space, _ in operands],
        out_specs=[space for space, _ in outs],
        scratch_shapes=list(scratch) + extra,
        compiler_params=pltpu.CompilerParams(vmem_limit_bytes=VMEM_LIMIT),
        cost_estimate=pl.CostEstimate(flops=flops, bytes_accessed=read, transcendentals=0),
    )(*[pltpu.with_memory_space_constraint(array, pltpu.HBM) if space is stored else array for space, array in operands])


def shape(dims, kind):
    return jax.ShapeDtypeStruct(dims, kind)


def exchange(block, axis):
    return lax.all_to_all(block, axis, split_axis=0, concat_axis=0, tiled=True)


def shards(
    patches,
    layer_norm_gain,
    layer_norm_bias,
    fc1_weight,
    fc1_bias,
    fc2_weight,
    counts,
    owners,
    text_embed,
    labels,
    logit_scale,
    logit_bias,
):
    dp_size = lax.axis_size("dp")
    mp_size = lax.axis_size("mp")
    dp_index = lax.axis_index("dp").astype(jnp.int32)[None]
    mp_index = lax.axis_index("mp").astype(jnp.int32)[None]
    loss_index = lax.axis_index("loss").astype(jnp.int32)[None]
    turn = jnp.where((mp_index + dp_index) % 2 == 0, 1, mp_size - 1)
    ring_place = jnp.concatenate([mp_index, turn])
    first_pairs, second_pairs = [], []
    for d in range(dp_size):
        for m in range(mp_size):
            step = 1 if (d + m) % 2 == 0 else mp_size - 1
            first_pairs.append((d * mp_size + m, d * mp_size + (m + step) % mp_size))
            second_pairs.append((d * mp_size + m, d * mp_size + (m - step) % mp_size))
    row_count, width = patches.shape
    hidden = fc1_weight.shape[1]
    share_rows = row_count // mp_size
    images = counts.shape[1]
    all_images = labels.shape[0]
    padded = -(-row_count // dp_size // 8) * 8
    fc1_t = fc1_weight.T
    matmul = 2 * row_count * width * hidden
    weight_bytes = 2 * width * hidden

    gain, bias, offset = layer_norm_gain, layer_norm_bias, fc1_bias
    gain_room, offset_room = pltpu.VMEM((width,), f32), pltpu.VMEM((hidden,), f32)
    plan_dims, counts_dims = owners.shape[1:], counts.shape
    first_room, second_room = pltpu.VMEM((hidden, width), bf16), pltpu.VMEM((hidden, width), bf16)

    (outgoing,) = call(
        functools.partial(pack_kernel, padded=padded),
        [(stored, shape((dp_size * padded, width), bf16))],
        [(scalars, dp_index), (stored, owners), (stored, patches)],
        [
            pltpu.SMEM(plan_dims, jnp.int32),
            pltpu.VMEM((row_count, width), bf16),
            pltpu.VMEM((dp_size * padded, width), bf16),
        ],
    )
    incoming = exchange(outgoing, "dp")

    patches, outgoing = lax.optimization_barrier((patches, outgoing))
    (partial_sums,) = call(
        functools.partial(pool_kernel, share=1.0 / mp_size),
        [(whole, shape((images, width), f32))],
        [(scalars, dp_index)]
        + [(stored, array) for array in (counts, patches, gain, bias, offset, fc1_t, fc2_weight)],
        [
            pltpu.SMEM(counts_dims, jnp.int32),
            pltpu.VMEM((row_count, width), bf16),
            gain_room,
            gain_room,
            offset_room,
            first_room,
            second_room,
        ],
        flops=matmul,
        read=2 * weight_bytes,
    )
    slab_sums = jnp.sum(lax.all_gather(partial_sums, "mp", axis=0), axis=0)
    incoming, slab_sums = lax.optimization_barrier((incoming, slab_sums))
    slope, own_rows, member, text_copies = call(
        slope_kernel,
        [
            (whole, shape((row_count, hidden), f32)),
            (whole, shape((share_rows, width), bf16)),
            (whole, shape((row_count, images), f32)),
            (whole, shape((all_images, width), bf16)),
        ],
        [(scalars, dp_index), (scalars, ring_place), (whole, incoming)]
        + [(stored, array) for array in (counts, owners, gain, bias, offset, text_embed, fc1_t)],
        [
            pltpu.SMEM(counts_dims, jnp.int32),
            pltpu.VMEM(plan_dims, jnp.int32),
            gain_room,
            gain_room,
            offset_room,
            pltpu.VMEM((images, width), bf16),
            first_room,
        ],
        flops=matmul,
        read=2 * weight_bytes,
    )
    texts = exchange(text_copies, "loss")
    slab_sums, slope = lax.optimization_barrier((slab_sums, slope))
    pieces = lax.all_gather(slab_sums, "dp", axis=0, tiled=True)
    upstream, parts, d_act, first_chunks = call(
        functools.partial(gradient_kernel, ring=mp_size),
        [
            (whole, shape((images, width), f32)),
            (stored, shape((all_images, width + LANES), bf16)),
            (whole, shape((2 * images, hidden), bf16)),
            (whole, shape((2 * share_rows, width), bf16)),
        ],
        [(scalars, array) for array in (loss_index, ring_place, logit_scale, logit_bias)]
        + [(whole, array) for array in (pieces, texts, member, slope)]
        + [(stored, array) for array in (counts, labels, fc2_weight, fc1_t)],
        [
            pltpu.SMEM(counts_dims, jnp.int32),
            pltpu.SMEM((all_images,), jnp.int32),
            second_room,
            first_room,
            pltpu.VMEM((all_images, width + LANES), bf16),
        ],
        flops=matmul,
        read=2 * weight_bytes,
    )
    first_received = lax.ppermute(first_chunks, ("dp", "mp"), first_pairs)
    factors = [(scalars, ring_place)] + [(whole, array) for array in (d_act, member, slope)]
    second_chunk, own_back = call(
        functools.partial(rest_kernel, ring=mp_size),
        [(whole, shape((share_rows, width), f32))] * 2,
        factors + [(stored, fc1_t)],
        [first_room],
        flops=matmul // 2,
        read=weight_bytes,
    )
    second_sum = (second_chunk + first_received[share_rows:].astype(f32)).astype(bf16)
    second_received = lax.ppermute(second_sum, ("dp", "mp"), second_pairs)
    all_parts = exchange(parts, "loss")
    grad_text, loss = call(
        text_kernel,
        [(whole, shape((images, width), f32)), (whole, shape((1, 1), f32))],
        [(whole, all_parts), (whole, text_embed)],
    )
    (grad_rows,) = call(
        functools.partial(row_kernel, ring=mp_size),
        [(whole, shape((share_rows, width), f32))],
        [(scalars, ring_place)]
        + [(whole, array) for array in (own_back, first_received, second_received, own_rows, member, upstream)]
        + [(stored, gain)],
        [gain_room],
    )
    return (grad_rows, grad_text, loss[0, 0])


def solution(mesh):
    placed = (
        P(("dp", "loss"), None),
        P(),
        P(),
        P(None, "mp"),
        P("mp"),
        P("mp", None),
        P("loss", None),
        P("loss", None, None),
        P("loss", None),
        P(),
        P(),
        P(),
    )
    return jax.shard_map(
        shards,
        mesh=mesh,
        in_specs=placed,
        out_specs=(P(("dp", "loss", "mp"), None), P("loss", None), P()),
        check_vma=False,
    )
```
